512 devices in a mesh: dp: 64 (over x, z), cent: 8 (over y, core).
Axes of the slice: x: 4, y: 4, z: 16, core: 2. Of those that a mesh axis runs over, the one named last changes fastest.
Arguments:
- points: bfloat16 [65536, 768], P('dp'), may hold values from -60 to 60
- centroids: bfloat16 [8192, 768], P('cent'), may hold values from -60 to 60
Outputs:
- new_centroids: bfloat16 [8192, 768], P('cent')
The draws below stay inside these ranges and needn't reach their ends.
All inputs are finite; a program needn't handle non-finite values.
Results may differ from the reference program's by a relative error of at most 0.0022.
Values may be sent and summed in bfloat16 or wider, within the bound.
A program may use at most 64 MiB of HBM per device.

```python
import math
import jax
import jax.numpy as jnp
from jax import lax

D = 768
K = 8192
PASSES = 3
NPTS = 65536


def shared_rows(key):
    base_key, scale_key = jax.random.split(jax.random.fold_in(key, 5))
    base = jnp.clip(jax.random.normal(base_key, (K, D), jnp.float32), -4.5, 4.5)
    spread = jnp.exp(jax.random.uniform(scale_key, (K, 1), jnp.float32, 0.0, math.log(10.0)))
    return (base, spread)


def draw_centroids(key, part):
    base, spread = shared_rows(key)
    return (base * spread).astype(jnp.bfloat16)


def draw_points(key, part):
    key = jax.random.fold_in(key, 23)
    scale_key, noise_key = jax.random.split(key, 2)
    row_scale = jnp.exp(jax.random.uniform(scale_key, (NPTS, 1), jnp.float32, math.log(0.3), math.log(3.0)))
    noise = jnp.clip(jax.random.normal(noise_key, (NPTS, D), jnp.float32), -4.5, 4.5)
    return (noise * row_scale).astype(jnp.bfloat16)


def setup_inputs(seed: int = 0) -> dict:
    key_of = jax.random.split(jax.random.key(seed), 3)
    points = draw_points(jax.random.fold_in(key_of[2], 71), 0)
    centroids = draw_centroids(jax.random.fold_in(key_of[2], 71), 0)
    return {"points": points, "centroids": centroids}


def reference(points, centroids):
    factor = 1.0 / math.sqrt(D)
    logits = jnp.dot(points, centroids.T, preferred_element_type=jnp.float32) * factor
    log_mass = math.log(NPTS / K)
    row_pot = jnp.zeros((NPTS,), jnp.float32)
    col_pot = jnp.zeros((K,), jnp.float32)
    for sweep in range(PASSES):
        col_pot = log_mass - jax.nn.logsumexp(logits + row_pot[:, None], axis=0)
        row_pot = -jax.nn.logsumexp(logits + col_pot[None, :], axis=1)
    weights = jnp.exp(logits + row_pot[:, None] + col_pot[None, :])
    mass = lax.optimization_barrier(jnp.sum(weights, axis=0))
    numerator = lax.dot_general(weights.astype(jnp.bfloat16), points, (((0,), (0,)), ((), ())), preferred_element_type=jnp.float32)
    updated = (numerator + centroids.astype(jnp.float32)) / (mass + 1.0)[:, None]
    return updated.astype(jnp.bfloat16)
```

```python
import functools
import math

import jax
import jax.numpy as jnp
from jax import lax
from jax.experimental import pallas as pl
from jax.experimental.pallas import tpu as pltpu
from jax.sharding import PartitionSpec as P

NX, NZ, NC = 4, 16, 8
LANES = 128
MESH = pl.DeviceIdType.MESH
FAR = [8, 7, 9, 6, 10, 5, 11, 4, 12, 3, 13, 2, 14, 1, 15]
NEAR = FAR[::-1]


def aligned(start, size):
    return pl.ds(pl.multiple_of(start, size), size)


def to_rows(wide, tiles):
    return jnp.concatenate(
        [wide[:, t * LANES : (t + 1) * LANES] for t in range(tiles)], axis=0
    )


def to_wide(rows, tiles):
    return jnp.concatenate([rows[t : t + 1, :] for t in range(tiles)], axis=1)


def kernel(
    log_mass, factor,
    p_ref, c_ref, o_ref,
    mat, scale, num, total, part,
    vec, cx, cz, rc, mx, nx, nz,
    vec_send, cx_recv, cz_recv, rc_recv, nx_send, nx_recv, nz_send, nz_recv, ag_send, agz_recv, agx_recv,
):
    npts, depth = p_ref.shape
    ncent = c_ref.shape[0]
    rt, ct = npts // LANES, ncent // LANES
    per_x, per = ncent // NX, ncent // (NX * NZ)

    dp = lax.axis_index("dp")
    cent = lax.axis_index("cent")
    x, z = dp // NZ, dp % NZ

    def x_peer(k):
        return {"dp": ((x + k) % NX) * NZ + z}

    def z_peer(k):
        return {"dp": x * NZ + (z + k) % NZ}

    def c_peer(k):
        return {"cent": (cent + k) % NC}

    x_peers = [x_peer(k) for k in range(1, NX)]
    z_peers = [z_peer(k) for k in range(1, NZ)]
    c_peers = [c_peer(k) for k in range(1, NC)]

    barrier = pltpu.get_barrier_semaphore()
    for peer in x_peers + z_peers + c_peers:
        pl.semaphore_signal(barrier, inc=1, device_id=peer, device_id_type=MESH)

    def swap(slot, rows, peers, land, recv):
        for k, peer in enumerate(peers):
            pltpu.make_async_remote_copy(
                src_ref=vec.at[slot, pl.ds(0, rows)],
                dst_ref=land.at[k, pl.ds(0, rows)],
                send_sem=vec_send.at[slot],
                recv_sem=recv,
                device_id=peer,
                device_id_type=MESH,
            ).start()

    def landed(land, recv):
        pltpu.make_async_copy(land, land, recv).wait()

    def merge(slot, land, count, tiles):
        peak = vec[slot, :tiles]
        for k in range(count):
            peak = jnp.maximum(peak, land[k, :tiles])
        acc = vec[slot, tiles : 2 * tiles] * jnp.exp(vec[slot, :tiles] - peak)
        for k in range(count):
            acc += land[k, tiles : 2 * tiles] * jnp.exp(land[k, :tiles] - peak)
        return peak, acc

    def add_up(slot, land, count, tiles):
        acc = vec[slot, :tiles]
        for k in range(count):
            acc += land[k, :tiles]
        return acc

    def spread(rows, tiles):
        for t in range(tiles):
            wide = jnp.broadcast_to(rows[t : t + 1, :], (LANES, LANES))
            scale[t * LANES : (t + 1) * LANES, :] = wide.T

    def column_sums():
        def step(r, acc):
            rows = aligned(r * LANES, LANES)
            by = scale[rows, :]
            out = []
            for t in range(ct):
                v = mat[rows, t * LANES : (t + 1) * LANES] * by
                out.append(acc[t] + jnp.sum(v.reshape(LANES // 8, 8, LANES), axis=0))
            return tuple(out)

        zero = tuple(jnp.zeros((8, LANES), jnp.float32) for _ in range(ct))
        acc = lax.fori_loop(0, rt, step, zero)
        return jnp.concatenate([jnp.sum(a, axis=0, keepdims=True) for a in acc], axis=0)

    def row_sums(wide):
        def step(r, carry):
            rows = aligned(r * LANES, LANES)
            acc = mat[rows, :LANES] * wide[:, :LANES]
            for t in range(1, ct):
                acc += mat[rows, t * LANES : (t + 1) * LANES] * wide[:, t * LANES : (t + 1) * LANES]
            part[pl.ds(r, 1), :] = jnp.sum(acc.T, axis=0, keepdims=True)
            return carry

        lax.fori_loop(0, rt, step, 0)

    def logits_step(r, peak):
        rows = aligned(r * 256, 256)
        got = factor * lax.dot_general(
            p_ref[rows, :], c_ref[...], (((1,), (1,)), ((), ())), preferred_element_type=jnp.float32
        )
        mat[rows, :] = got
        return jnp.maximum(peak, jnp.max(got.reshape(32, 8, ncent), axis=0))

    peak8 = lax.fori_loop(
        0, npts // 256, logits_step, jnp.full((8, ncent), -jnp.inf, jnp.float32)
    )
    peak = jnp.max(peak8, axis=0, keepdims=True)

    def first_sum(r, acc):
        rows = aligned(r * LANES, LANES)
        got = jnp.exp(mat[rows, :] - peak)
        return acc + jnp.sum(got.reshape(LANES // 8, 8, ncent), axis=0)

    acc = lax.fori_loop(0, rt, first_sum, jnp.zeros((8, ncent), jnp.float32))
    vec[0, :ct] = to_rows(peak, ct)
    vec[0, ct : 2 * ct] = to_rows(jnp.sum(acc, axis=0, keepdims=True), ct)

    pl.semaphore_wait(barrier, NX + NZ + NC - 3)

    swap(0, 2 * ct, x_peers, cx.at[0], cx_recv.at[0])
    landed(cx.at[0], cx_recv.at[0])
    m, s = merge(0, cx.at[0], NX - 1, ct)
    vec[1, :ct] = m
    vec[1, ct : 2 * ct] = s
    swap(1, 2 * ct, z_peers, cz.at[0], cz_recv.at[0])
    landed(cz.at[0], cz_recv.at[0])
    m, s = merge(1, cz.at[0], NZ - 1, ct)
    col_pot = to_wide(log_mass - (m + jnp.log(s)), ct)

    def first_rows(r, carry):
        rows = aligned(r * LANES, LANES)
        got = mat[rows, :] + col_pot
        top = got[:, :LANES]
        for t in range(1, ct):
            top = jnp.maximum(top, got[:, t * LANES : (t + 1) * LANES])
        top = jnp.max(top, axis=1, keepdims=True)
        got = jnp.exp(got - top)
        mat[rows, :] = got
        acc = got[:, :LANES]
        for t in range(1, ct):
            acc += got[:, t * LANES : (t + 1) * LANES]
        part[pl.ds(r, 1), :] = jnp.sum(acc.T, axis=0, keepdims=True)
        vec[2, pl.ds(r, 1), :] = jnp.broadcast_to(top, (LANES, LANES)).T[:1, :]
        return carry

    lax.fori_loop(0, rt, first_rows, 0)
    vec[2, rt : 2 * rt] = part[...]
    swap(2, 2 * rt, c_peers, rc.at[0], rc_recv.at[0])
    landed(rc.at[0], rc_recv.at[0])
    m, s = merge(2, rc.at[0], NC - 1, rt)
    u = jnp.exp(vec[2, :rt] - (m + jnp.log(s)))
    v = None
    spread(u, rt)

    slot = 3
    for sweep in (1, 2):
        vec[slot, :ct] = column_sums()
        swap(slot, ct, x_peers, cx.at[sweep, :, pl.ds(0, ct)], cx_recv.at[sweep])
        landed(cx.at[sweep, :, pl.ds(0, ct)], cx_recv.at[sweep])
        vec[slot + 1, :ct] = add_up(slot, cx.at[sweep], NX - 1, ct)
        swap(slot + 1, ct, z_peers, cz.at[sweep, :, pl.ds(0, ct)], cz_recv.at[sweep])
        landed(cz.at[sweep, :, pl.ds(0, ct)], cz_recv.at[sweep])
        v = math.exp(log_mass) / add_up(slot + 1, cz.at[sweep], NZ - 1, ct)
        row_sums(to_wide(v, ct))
        vec[slot + 2, :rt] = u * part[...]
        swap(slot + 2, rt, c_peers, rc.at[sweep, :, pl.ds(0, rt)], rc_recv.at[sweep])
        landed(rc.at[sweep, :, pl.ds(0, rt)], rc_recv.at[sweep])
        u = u / add_up(slot + 2, rc.at[sweep], NC - 1, rt)
        spread(u, rt)
        slot += 3

    vec[slot, :ct] = v * column_sums()
    swap(slot, ct, x_peers, mx.at[pl.ds(0, NX - 1)], cx_recv.at[3])
    for t in range(ct):
        total[t : t + 1, :] = v[t : t + 1, :]

    def to_x(j, to):
        rows = ((to * NZ + (z + j) % NZ)) * per
        return num.at[aligned(rows, per)]

    for k in (2, 1, 3, 0):
        to = (x + k) % NX
        cols = aligned(to * per_x, per_x)
        wide = to_wide(total[pl.ds(to * (per_x // LANES), per_x // LANES), :], per_x // LANES)
        weights = []
        for r in range(rt):
            by = scale[r * LANES : (r + 1) * LANES, :]
            got = mat[r * LANES : (r + 1) * LANES, cols]
            weights.append(
                jnp.concatenate(
                    [
                        got[:, t * LANES : (t + 1) * LANES] * by * wide[:, t * LANES : (t + 1) * LANES]
                        for t in range(per_x // LANES)
                    ],
                    axis=1,
                ).astype(jnp.bfloat16)
            )
        num[cols, :] = lax.dot_general(
            jnp.concatenate(weights, axis=0), p_ref[...],
            (((0,), (0,)), ((), ())), preferred_element_type=jnp.float32,
        )
        if k:
            for j in FAR + [0]:
                pltpu.make_async_remote_copy(
                    src_ref=to_x(j, to),
                    dst_ref=nx.at[j, k - 1],
                    send_sem=nx_send,
                    recv_sem=nx_recv.at[j],
                    device_id=x_peer(k),
                    device_id_type=MESH,
                ).start()

    landed(mx.at[pl.ds(0, NX - 1)], cx_recv.at[3])
    vec[slot + 1, :ct] = add_up(slot, mx, NX - 1, ct)
    swap(slot + 1, ct, z_peers, mx.at[pl.ds(NX - 1, NZ - 1)], cz_recv.at[3])

    for j in FAR + [0]:
        landed(nx.at[j], nx_recv.at[j])
        mine = to_x(j, x)
        mine[...] = mine[...] + nx[j, 0] + nx[j, 1] + nx[j, 2]
        if j:
            pltpu.make_async_remote_copy(
                src_ref=mine,
                dst_ref=nz.at[j - 1],
                send_sem=nz_send,
                recv_sem=nz_recv,
                device_id=z_peer(j),
                device_id_type=MESH,
            ).start()

    landed(mx.at[pl.ds(NX - 1, NZ - 1)], cz_recv.at[3])
    mass = vec[slot + 1, :ct]
    for k in range(NX - 1, NX + NZ - 2):
        mass += mx[k]
    total[...] = mass
    first = (x * NZ + z) * per
    row = total[pl.ds(first // LANES, 1), :]
    scale[:LANES, :] = jnp.broadcast_to(row, (LANES, LANES)).T
    mass = scale[aligned(first % LANES, per), :][:, :1]

    landed(nz, nz_recv)
    own = aligned(first, per)
    acc = num[own, :]
    for k in range(NZ - 1):
        acc += nz[k]
    acc = (acc + c_ref[own, :].astype(jnp.float32)) / (mass + 1.0)
    o_ref[own, :] = acc.astype(o_ref.dtype)

    def send_rows(rows, peer, recv):
        pltpu.make_async_remote_copy(
            src_ref=o_ref.at[rows], dst_ref=o_ref.at[rows],
            send_sem=ag_send, recv_sem=recv, device_id=peer, device_id_type=MESH,
        ).start()

    for j in FAR:
        send_rows(own, z_peer(j), agz_recv.at[j - 1])
    for j in [0] + NEAR:
        rows = aligned((x * NZ + (z + NZ - j) % NZ) * per, per)
        if j:
            landed(o_ref.at[rows], agz_recv.at[j - 1])
        for k in (2, 1, 3):
            send_rows(rows, x_peer(k), agx_recv)

    rest = o_ref.at[pl.ds(0, (NX - 1) * per_x)]
    landed(rest, agx_recv)

    for sweep in range(3):
        rows = 2 * ct if sweep == 0 else ct
        landed(cx.at[sweep, :, pl.ds(0, rows)], vec_send.at[3 * sweep])
        landed(cz.at[sweep, :, pl.ds(0, rows)], vec_send.at[3 * sweep + 1])
        landed(rc.at[sweep, :, pl.ds(0, rows)], vec_send.at[3 * sweep + 2])
    landed(mx.at[pl.ds(0, NX - 1)], vec_send.at[slot])
    landed(mx.at[pl.ds(NX - 1, NZ - 1)], vec_send.at[slot + 1])
    landed(num.at[pl.ds(0, (NX - 1) * per_x)], nx_send)
    landed(nz, nz_send)
    landed(o_ref.at[pl.ds(0, (NZ - 1) * per)], ag_send)
    landed(rest, ag_send)


def shards(points, centroids):
    npts, depth = points.shape
    ncent = centroids.shape[0]
    n_total = npts * lax.axis_size("dp")
    k_total = ncent * lax.axis_size("cent")
    tiles = max(npts, ncent) // LANES
    per = ncent // (NX * NZ)
    f32 = jnp.float32
    vmem = pl.BlockSpec(memory_space=pltpu.VMEM)
    dma = pltpu.SemaphoreType.DMA
    return pl.pallas_call(
        functools.partial(kernel, math.log(n_total / k_total), 1.0 / math.sqrt(depth)),
        out_shape=jax.ShapeDtypeStruct((ncent, depth), jnp.bfloat16),
        in_specs=[vmem, vmem],
        out_specs=vmem,
        scratch_shapes=[
            pltpu.VMEM((npts, ncent), f32),
            pltpu.VMEM((max(npts, ncent), LANES), f32),
            pltpu.VMEM((ncent, depth), f32),
            pltpu.VMEM((tiles, LANES), f32),
            pltpu.VMEM((npts // LANES, LANES), f32),
            pltpu.VMEM((11, 2 * tiles, LANES), f32),
            pltpu.VMEM((3, NX - 1, 2 * tiles, LANES), f32),
            pltpu.VMEM((3, NZ - 1, 2 * tiles, LANES), f32),
            pltpu.VMEM((3, NC - 1, 2 * tiles, LANES), f32),
            pltpu.VMEM((NX + NZ - 2, ncent // LANES, LANES), f32),
            pltpu.VMEM((NZ, NX - 1, per, depth), f32),
            pltpu.VMEM((NZ - 1, per, depth), f32),
            dma((11,)), dma((4,)), dma((4,)), dma((3,)),
            dma, dma((NZ,)), dma, dma, dma, dma((NZ - 1,)), dma,
        ],
        compiler_params=pltpu.CompilerParams(
            collective_id=0, has_side_effects=True, vmem_limit_bytes=48 * 2**20
        ),
        cost_estimate=pl.CostEstimate(
            flops=4 * npts * ncent * depth, transcendentals=2 * npts * ncent,
            bytes_accessed=2 * (npts + 2 * ncent) * depth,
        ),
        name="balance",
    )(points, centroids)


def solution(mesh):
    return jax.shard_map(
        shards,
        mesh=mesh,
        in_specs=(P("dp", None), P("cent", None)),
        out_specs=P("cent", None),
        check_vma=False,
    )
```

```python
import functools
import math

import jax
import jax.numpy as jnp
from jax import lax
from jax.experimental import pallas as pl
from jax.experimental.pallas import tpu as pltpu
from jax.sharding import PartitionSpec as P

NX, NZ, NC = 4, 16, 8
LANES = 128
MESH = pl.DeviceIdType.MESH
FAR = [8, 7, 9, 6, 10, 5, 11, 4, 12, 3, 13, 2, 14, 1, 15]
NEAR = [3, 13, 2, 14, 1, 15]
BY_RELAY = [8, 9, 7, 10, 6, 11, 5]
LANDING = [0, 4, 12, 1, 15, 2, 14, 3, 13, 5, 11, 6, 10, 7, 9, 8]


def aligned(start, size):
    return pl.ds(pl.multiple_of(start, size), size)


def to_rows(wide, tiles):
    return jnp.concatenate(
        [wide[:, t * LANES : (t + 1) * LANES] for t in range(tiles)], axis=0
    )


def to_wide(rows, tiles):
    return jnp.concatenate([rows[t : t + 1, :] for t in range(tiles)], axis=1)


def kernel(
    log_mass, factor,
    p_hbm, c_hbm, o_ref,
    p_ref, c_ref, pts, mat, scale, tile, num, total, part, top, cpot,
    vec, cx, cz, rc, px, mass_out, mass_in, nz,
    in_sem, pts_send, pts_recv, pair_send, pair_recv,
    vec_send, cx_recv, cz_recv, rc_recv, px_recv, mass_send, mass_recv,
    nz_send, nz_recv, ag_send, agz_recv, agl_recv, agr_recv, agx_recv,
):
    npts, depth = p_ref.shape
    ncent = c_ref.shape[0]
    rt, ct = npts // LANES, ncent // LANES
    per_x, per = ncent // NX, ncent // (NX * NZ)
    qt = per_x // LANES
    half = npts // 2
    f32 = jnp.float32

    dp = lax.axis_index("dp")
    cent = lax.axis_index("cent")
    x, z = dp // NZ, dp % NZ
    core = cent % 2

    def x_peer(k):
        return {"dp": ((x + k) % NX) * NZ + z}

    def z_peer(k):
        return {"dp": x * NZ + (z + k) % NZ}

    def c_peer(k):
        return {"cent": (cent + k) % NC}

    sibling = {"cent": cent + 1 - 2 * core}
    x_peers = [x_peer(k) for k in range(1, NX)]
    z_peers = [z_peer(k) for k in range(1, NZ)]
    c_peers = [c_peer(k) for k in range(1, NC)]

    c_in = pltpu.make_async_copy(c_hbm, c_ref, in_sem.at[4])
    c_in.start()
    p_in = []
    for r in range(4):
        rows = pl.ds(r * (npts // 4), npts // 4)
        p_in.append(pltpu.make_async_copy(p_hbm.at[rows], p_ref.at[rows], in_sem.at[r]))
        p_in[-1].start()

    barrier = pltpu.get_barrier_semaphore()
    for peer in x_peers + z_peers + c_peers:
        pl.semaphore_signal(barrier, inc=1, device_id=peer, device_id_type=MESH)

    pending = []

    def send(src, dst, send_sem, recv_sem, peer):
        pltpu.make_async_remote_copy(
            src_ref=src, dst_ref=dst, send_sem=send_sem, recv_sem=recv_sem,
            device_id=peer, device_id_type=MESH,
        ).start()

    def landed(land, recv):
        pltpu.make_async_copy(land, land, recv).wait()

    def drain():
        for land, sem in pending:
            landed(land, sem)

    def swap(src, peers, land, send_sem, recv, order=None):
        for k in order or range(1, len(peers) + 1):
            send(src, land.at[k - 1], send_sem, recv, peers[k - 1])
        pending.append((land, send_sem))

    def merge(own, land, count):
        peak = own
        for k in range(count):
            peak = jnp.maximum(peak, land[k])
        acc = jnp.exp(own - peak)
        for k in range(count):
            acc += jnp.exp(land[k] - peak)
        return peak + jnp.log(acc)

    def add_up(own, land, count):
        acc = own
        for k in range(count):
            acc += land[k]
        return acc

    def spread(rows, out, tiles):
        for t in range(tiles):
            wide = jnp.broadcast_to(rows[t : t + 1, :], (LANES, LANES))
            out[t * LANES : (t + 1) * LANES, :] = wide.T

    def column_sums():
        def step(r, acc):
            rows = aligned(r * LANES, LANES)
            by = scale[rows, :]
            out = []
            for t in range(ct):
                v = mat[rows, t * LANES : (t + 1) * LANES] * by
                out.append(acc[t] + jnp.sum(v.reshape(LANES // 8, 8, LANES), axis=0))
            return tuple(out)

        zero = tuple(jnp.zeros((8, LANES), f32) for _ in range(ct))
        acc = lax.fori_loop(0, rt, step, zero)
        return jnp.concatenate([jnp.sum(a, axis=0, keepdims=True) for a in acc], axis=0)

    def row_sums(wide):
        def step(r, carry):
            rows = aligned(r * LANES, LANES)
            acc = mat[rows, :LANES] * wide[:, :LANES]
            for t in range(1, ct):
                acc += mat[rows, t * LANES : (t + 1) * LANES] * wide[:, t * LANES : (t + 1) * LANES]
            part[pl.ds(r, 1), :] = jnp.sum(acc.T, axis=0, keepdims=True)
            return carry

        lax.fori_loop(0, rt, step, 0)

    c_in.wait()
    peak8 = jnp.full((8, ncent), -jnp.inf, f32)
    for r in range(4):
        p_in[r].wait()
        rows = pl.ds(r * (npts // 4), npts // 4)
        got = factor * lax.dot_general(
            p_ref[rows, :], c_ref[...], (((1,), (1,)), ((), ())), preferred_element_type=f32
        )
        mat[rows, :] = got
        peak8 = jnp.maximum(peak8, jnp.max(got.reshape(npts // 32, 8, ncent), axis=0))
    peak = jnp.max(peak8, axis=0, keepdims=True)

    def first_sum(r, acc):
        rows = aligned(r * LANES, LANES)
        got = jnp.exp(mat[rows, :] - peak)
        return acc + jnp.sum(got.reshape(LANES // 8, 8, ncent), axis=0)

    acc = lax.fori_loop(0, rt, first_sum, jnp.zeros((8, ncent), f32))
    vec[0] = to_rows(peak + jnp.log(jnp.sum(acc, axis=0, keepdims=True)), ct)

    pl.semaphore_wait(barrier, NX + NZ + NC - 3)

    swap(vec.at[0], x_peers, cx.at[0], vec_send.at[0], cx_recv.at[0])

    mine = aligned(core * half, half)
    for k in (1, 3, 2):
        send(p_ref.at[mine], pts.at[k - 1, mine], pts_send, pts_recv.at[k - 1], x_peers[k - 1])
    pending.append((pts.at[:, mine], pts_send))

    def pass_on(k):
        landed(pts.at[k - 1, mine], pts_recv.at[k - 1])
        send(pts.at[k - 1, mine], pts.at[k - 1, mine], pair_send, pair_recv, sibling)

    landed(cx.at[0], cx_recv.at[0])
    vec[1] = merge(vec[0], cx.at[0], NX - 1)
    swap(vec.at[1], z_peers, cz.at[0], vec_send.at[1], cz_recv.at[0], FAR)
    landed(cz.at[0], cz_recv.at[0])
    col_pot = log_mass - merge(vec[1], cz.at[0], NZ - 1)
    wide_pot = to_wide(col_pot, ct)

    def first_rows(r, carry):
        rows = aligned(r * LANES, LANES)
        got = mat[rows, :] + wide_pot
        high = got[:, :LANES]
        for t in range(1, ct):
            high = jnp.maximum(high, got[:, t * LANES : (t + 1) * LANES])
        high = jnp.max(high, axis=1, keepdims=True)
        got = jnp.exp(got - high)
        mat[rows, :] = got
        acc = got[:, :LANES]
        for t in range(1, ct):
            acc += got[:, t * LANES : (t + 1) * LANES]
        part[pl.ds(r, 1), :] = jnp.sum(acc.T, axis=0, keepdims=True)
        top[pl.ds(r, 1), :] = jnp.broadcast_to(high, (LANES, LANES)).T[:1, :]
        return carry

    lax.fori_loop(0, rt, first_rows, 0)
    vec[2] = top[...] + jnp.log(part[...])
    swap(vec.at[2], c_peers, rc.at[0], vec_send.at[2], rc_recv.at[0])
    landed(rc.at[0], rc_recv.at[0])
    row_pot = -merge(vec[2], rc.at[0], NC - 1)
    u = jnp.exp(top[...] + row_pot)
    spread(u, scale, rt)

    for sweep in (1, 2):
        at = 3 * sweep
        vec[at] = column_sums()
        swap(vec.at[at], x_peers, cx.at[sweep], vec_send.at[at], cx_recv.at[sweep])
        landed(cx.at[sweep], cx_recv.at[sweep])
        vec[at + 1] = add_up(vec[at], cx.at[sweep], NX - 1)
        swap(vec.at[at + 1], z_peers, cz.at[sweep], vec_send.at[at + 1], cz_recv.at[sweep], FAR)
        if sweep == 1:
            pass_on(1)
            pass_on(3)
        else:
            pass_on(2)
            pending.append((pts.at[:, mine], pair_send))
            landed(pts.at[:, aligned(half - core * half, half)], pair_recv)
            quarter = c_ref[aligned(x * per_x, per_x), :]
            for k in range(NX):
                tile[:, k * npts : (k + 1) * npts] = factor * lax.dot_general(
                    quarter, p_ref[...] if k == 0 else pts[k - 1],
                    (((1,), (1,)), ((), ())), preferred_element_type=f32,
                )
            landed(px.at[0], px_recv.at[0])
        landed(cz.at[sweep], cz_recv.at[sweep])
        v = math.exp(log_mass) / add_up(vec[at + 1], cz.at[sweep], NZ - 1)
        row_sums(to_wide(v, ct))
        vec[at + 2] = u * part[...]
        swap(vec.at[at + 2], c_peers, rc.at[sweep], vec_send.at[at + 2], rc_recv.at[sweep])
        if sweep == 2:
            total[...] = col_pot + jnp.log(v)
            spread(total[pl.ds(x * qt, qt), :], cpot, qt)
            for k in range(NX):
                pot = vec[9] if k == 0 else px[0, k - 1]
                for t in range(rt):
                    cols = slice(k * npts + t * LANES, k * npts + (t + 1) * LANES)
                    tile[:, cols] = jnp.exp(tile[:, cols] + (cpot[...] + pot[t : t + 1, :]))
        landed(rc.at[sweep], rc_recv.at[sweep])
        got = add_up(vec[at + 2], rc.at[sweep], NC - 1)
        if sweep == 1:
            u = u / got
            vec[9] = row_pot - jnp.log(got)
            swap(vec.at[9], x_peers, px.at[0], vec_send.at[9], px_recv.at[0])
            spread(u, scale, rt)
        else:
            vec[10] = 1.0 / got
            swap(vec.at[10], x_peers, px.at[1], vec_send.at[10], px_recv.at[1])
            landed(px.at[1], px_recv.at[1])

    mass = jnp.zeros((per_x, LANES), f32)
    acc = jnp.zeros((per_x, depth), f32)
    for k in range(NX):
        by = vec[10] if k == 0 else px[1, k - 1]
        weights = []
        for t in range(rt):
            got = tile[:, k * npts + t * LANES : k * npts + (t + 1) * LANES] * by[t : t + 1, :]
            mass += got
            weights.append(got.astype(jnp.bfloat16))
        acc += jnp.dot(
            jnp.concatenate(weights, axis=1), p_ref[...] if k == 0 else pts[k - 1],
            preferred_element_type=f32,
        )
    num[...] = acc

    def piece(j):
        return num.at[aligned(((z + j) % NZ) * per, per)]

    for j in BY_RELAY:
        by = j - 4 if j < 8 else j + 4
        send(piece(j), nz.at[j - 1], nz_send, nz_recv.at[1 if j < 8 else 2], z_peers[by - 1])
    for j in NEAR:
        send(piece(j), nz.at[j - 1], nz_send, nz_recv.at[0], z_peers[j - 1])
    for t in range(qt):
        mass_out[t : t + 1, :] = jnp.sum(mass[t * LANES : (t + 1) * LANES, :].T, axis=0, keepdims=True)
    swap(mass_out, z_peers, mass_in, mass_send, mass_recv, FAR)
    for j, group, slots in ((4, 1, (5, 6, 7)), (12, 2, (8, 9, 10, 11))):
        landed(nz.at[pl.ds(slots[0] - 1, len(slots))], nz_recv.at[group])
        here = piece(j)
        acc = here[...]
        for i in slots:
            acc += nz[i - 1]
        here[...] = acc
        send(here, nz.at[j - 1], nz_send, nz_recv.at[0], z_peers[j - 1])
    pending.append((nz, nz_send))

    landed(mass_in, mass_recv)
    total[:qt, :] = add_up(mass_out[...], mass_in, NZ - 1)
    row = total[pl.ds(z * per // LANES, 1), :]
    scale[:LANES, :] = jnp.broadcast_to(row, (LANES, LANES)).T
    mass = scale[aligned((z * per) % LANES, per), :][:, :1]

    landed(nz.at[pl.ds(0, 8)], nz_recv.at[0])
    acc = piece(0)[...]
    for j in NEAR + [4, 12]:
        acc += nz[j - 1]
    own = aligned((x * NZ + z) * per, per)
    acc = (acc + c_ref[own, :].astype(f32)) / (mass + 1.0)
    o_ref[own, :] = acc.astype(o_ref.dtype)

    def rows_of(i, j):
        return o_ref.at[aligned((((x + i) % NX) * NZ + (z + NZ - j) % NZ) * per, per)]

    def hand_on(rows, recv, peer):
        send(rows, rows, ag_send, recv, peer)

    for j in (4, 12, 1, 15, 2, 14, 3, 13):
        hand_on(rows_of(0, 0), agz_recv.at[j], z_peers[j - 1])

    def relay(n):
        j = LANDING[n]
        if n % 2:
            landed(rows_of(1, j), agr_recv.at[j])
            hand_on(rows_of(1, j), agx_recv, x_peers[2])
        else:
            landed(rows_of(3, j), agl_recv.at[j])
            hand_on(rows_of(3, j), agx_recv, x_peers[0])

    lag = 2
    for n, j in enumerate(LANDING):
        rows = rows_of(0, j)
        if j:
            landed(rows, agz_recv.at[j])
        if j == 4:
            for a in (4, 3, 2, 1):
                hand_on(rows, agz_recv.at[4 + a], z_peers[a - 1])
        if j == 12:
            for a in (3, 2, 1):
                hand_on(rows, agz_recv.at[12 - a], z_peers[NZ - a - 1])
        hand_on(rows, agx_recv if n % 2 else agl_recv.at[j], x_peers[0])
        hand_on(rows, agr_recv.at[j] if n % 2 else agx_recv, x_peers[2])
        if n >= lag:
            relay(n - lag)
    for n in range(NZ - lag, NZ):
        relay(n)
    landed(o_ref.at[pl.ds(0, 2 * NZ * per)], agx_recv)
    pending.append((o_ref.at[pl.ds(0, (4 * NZ - 1) * per)], ag_send))

    drain()


def shards(points, centroids):
    npts, depth = points.shape
    ncent = centroids.shape[0]
    n_total = npts * lax.axis_size("dp")
    k_total = ncent * lax.axis_size("cent")
    rt, ct = npts // LANES, ncent // LANES
    per_x, per = ncent // NX, ncent // (NX * NZ)
    f32, bf16 = jnp.float32, jnp.bfloat16
    vmem = pl.BlockSpec(memory_space=pltpu.VMEM)
    hbm = pl.BlockSpec(memory_space=pl.ANY)
    dma = pltpu.SemaphoreType.DMA
    return pl.pallas_call(
        functools.partial(kernel, math.log(n_total / k_total), 1.0 / math.sqrt(depth)),
        out_shape=jax.ShapeDtypeStruct((ncent, depth), bf16),
        in_specs=[hbm, hbm],
        out_specs=vmem,
        scratch_shapes=[
            pltpu.VMEM((npts, depth), bf16),
            pltpu.VMEM((ncent, depth), bf16),
            pltpu.VMEM((NX - 1, npts, depth), bf16),
            pltpu.VMEM((npts, ncent), f32),
            pltpu.VMEM((npts, LANES), f32),
            pltpu.VMEM((per_x, NX * npts), f32),
            pltpu.VMEM((per_x, depth), f32),
            pltpu.VMEM((ct, LANES), f32),
            pltpu.VMEM((rt, LANES), f32),
            pltpu.VMEM((rt, LANES), f32),
            pltpu.VMEM((per_x, LANES), f32),
            pltpu.VMEM((11, ct, LANES), f32),
            pltpu.VMEM((3, NX - 1, ct, LANES), f32),
            pltpu.VMEM((3, NZ - 1, ct, LANES), f32),
            pltpu.VMEM((3, NC - 1, rt, LANES), f32),
            pltpu.VMEM((2, NX - 1, rt, LANES), f32),
            pltpu.VMEM((per_x // LANES, LANES), f32),
            pltpu.VMEM((NZ - 1, per_x // LANES, LANES), f32),
            pltpu.VMEM((NZ - 1, per, depth), f32),
            dma((5,)), dma, dma((NX - 1,)), dma, dma,
            dma((11,)), dma((3,)), dma((3,)), dma((3,)), dma((2,)), dma, dma,
            dma, dma((3,)), dma, dma((NZ,)), dma((NZ,)), dma((NZ,)), dma,
        ],
        compiler_params=pltpu.CompilerParams(
            collective_id=0, has_side_effects=True, vmem_limit_bytes=48 * 2**20
        ),
        cost_estimate=pl.CostEstimate(
            flops=6 * npts * ncent * depth, transcendentals=3 * npts * ncent,
            bytes_accessed=2 * (npts + 2 * ncent) * depth,
        ),
        name="balance",
    )(points, centroids)


def solution(mesh):
    return jax.shard_map(
        shards,
        mesh=mesh,
        in_specs=(P("dp", None), P("cent", None)),
        out_specs=P("cent", None),
        check_vma=False,
    )
```

```python
import functools
import math

import jax
import jax.numpy as jnp
from jax import lax
from jax.experimental import pallas as pl
from jax.experimental.pallas import tpu as pltpu
from jax.sharding import PartitionSpec as P

NX, NZ, NC = 4, 16, 8
LANES = 128
MESH = pl.DeviceIdType.MESH
FAR = [8, 7, 9, 6, 10, 5, 11, 4, 12, 3, 13, 2, 14, 1, 15]
NEAR = [3, 13, 2, 14, 1, 15]
BY_RELAY = [8, 9, 7, 10, 6, 11, 5]
LANDING = [0, 4, 12, 1, 15, 2, 14, 3, 13, 5, 11, 6, 10, 7, 9, 8]


def aligned(start, size):
    return pl.ds(pl.multiple_of(start, size), size)


def to_rows(wide, tiles):
    return jnp.concatenate(
        [wide[:, t * LANES : (t + 1) * LANES] for t in range(tiles)], axis=0
    )


def to_wide(rows, tiles):
    return jnp.concatenate([rows[t : t + 1, :] for t in range(tiles)], axis=1)


def kernel(
    log_mass, factor,
    p_hbm, c_hbm, o_ref,
    p_ref, c_ref, pts, mat, scale, tile, num, total, part, top, cpot,
    vec, cx, cz, rc, px, mass_out, mass_in, nz,
    in_sem, pts_send, pts_recv, pair_send, pair_recv,
    vec_send, cx_recv, cz_recv, rc_recv, px_recv, mass_send, mass_recv,
    nz_send, nz_recv, ag_send, agz_recv, agx_recv,
):
    npts, depth = p_ref.shape
    ncent = c_ref.shape[0]
    rt, ct = npts // LANES, ncent // LANES
    per_x, per = ncent // NX, ncent // (NX * NZ)
    qt = per_x // LANES
    half = npts // 2
    f32 = jnp.float32

    dp = lax.axis_index("dp")
    cent = lax.axis_index("cent")
    x, z = dp // NZ, dp % NZ
    core = cent % 2

    def x_peer(k):
        return {"dp": ((x + k) % NX) * NZ + z}

    def z_peer(k):
        return {"dp": x * NZ + (z + k) % NZ}

    def c_peer(k):
        return {"cent": (cent + k) % NC}

    sibling = {"cent": cent + 1 - 2 * core}
    x_peers = [x_peer(k) for k in range(1, NX)]
    z_peers = [z_peer(k) for k in range(1, NZ)]
    c_peers = [c_peer(k) for k in range(1, NC)]

    c_in = pltpu.make_async_copy(c_hbm, c_ref, in_sem.at[4])
    c_in.start()
    p_in = []
    for r in range(4):
        rows = pl.ds(r * (npts // 4), npts // 4)
        p_in.append(pltpu.make_async_copy(p_hbm.at[rows], p_ref.at[rows], in_sem.at[r]))
        p_in[-1].start()

    barrier = pltpu.get_barrier_semaphore()
    for peer in x_peers + z_peers + c_peers:
        pl.semaphore_signal(barrier, inc=1, device_id=peer, device_id_type=MESH)

    pending = []

    def send(src, dst, send_sem, recv_sem, peer):
        pltpu.make_async_remote_copy(
            src_ref=src, dst_ref=dst, send_sem=send_sem, recv_sem=recv_sem,
            device_id=peer, device_id_type=MESH,
        ).start()

    def landed(land, recv):
        pltpu.make_async_copy(land, land, recv).wait()

    def drain():
        for land, sem in pending:
            landed(land, sem)

    def swap(src, peers, land, send_sem, recv, order=None):
        for k in order or range(1, len(peers) + 1):
            send(src, land.at[k - 1], send_sem, recv, peers[k - 1])
        pending.append((land, send_sem))

    def merge(own, land, count):
        peak = own
        for k in range(count):
            peak = jnp.maximum(peak, land[k])
        acc = jnp.exp(own - peak)
        for k in range(count):
            acc += jnp.exp(land[k] - peak)
        return peak + jnp.log(acc)

    def add_up(own, land, count):
        acc = own
        for k in range(count):
            acc += land[k]
        return acc

    def spread(rows, out, tiles):
        for t in range(tiles):
            wide = jnp.broadcast_to(rows[t : t + 1, :], (LANES, LANES))
            out[t * LANES : (t + 1) * LANES, :] = wide.T

    def column_sums():
        def step(r, acc):
            rows = aligned(r * LANES, LANES)
            by = scale[rows, :]
            out = []
            for t in range(ct):
                v = mat[rows, t * LANES : (t + 1) * LANES] * by
                out.append(acc[t] + jnp.sum(v.reshape(LANES // 8, 8, LANES), axis=0))
            return tuple(out)

        zero = tuple(jnp.zeros((8, LANES), f32) for _ in range(ct))
        acc = lax.fori_loop(0, rt, step, zero)
        return jnp.concatenate([jnp.sum(a, axis=0, keepdims=True) for a in acc], axis=0)

    def row_sums(wide):
        def step(r, carry):
            rows = aligned(r * LANES, LANES)
            acc = mat[rows, :LANES] * wide[:, :LANES]
            for t in range(1, ct):
                acc += mat[rows, t * LANES : (t + 1) * LANES] * wide[:, t * LANES : (t + 1) * LANES]
            part[pl.ds(r, 1), :] = jnp.sum(acc.T, axis=0, keepdims=True)
            return carry

        lax.fori_loop(0, rt, step, 0)

    c_in.wait()
    peak8 = jnp.full((8, ncent), -jnp.inf, f32)
    for r in range(4):
        p_in[r].wait()
        rows = pl.ds(r * (npts // 4), npts // 4)
        got = factor * lax.dot_general(
            p_ref[rows, :], c_ref[...], (((1,), (1,)), ((), ())), preferred_element_type=f32
        )
        mat[rows, :] = got
        peak8 = jnp.maximum(peak8, jnp.max(got.reshape(npts // 32, 8, ncent), axis=0))
    peak = jnp.max(peak8, axis=0, keepdims=True)

    def first_sum(r, acc):
        rows = aligned(r * LANES, LANES)
        got = jnp.exp(mat[rows, :] - peak)
        return acc + jnp.sum(got.reshape(LANES // 8, 8, ncent), axis=0)

    acc = lax.fori_loop(0, rt, first_sum, jnp.zeros((8, ncent), f32))
    vec[0] = to_rows(peak + jnp.log(jnp.sum(acc, axis=0, keepdims=True)), ct)

    pl.semaphore_wait(barrier, NX + NZ + NC - 3)

    swap(vec.at[0], x_peers, cx.at[0], vec_send.at[0], cx_recv.at[0])

    mine = aligned(core * half, half)
    parts = (aligned(core * half, half // 2), aligned(core * half + half // 2, half // 2))

    def fetch():
        for k in (1, 3):
            send(p_ref.at[mine], pts.at[k - 1, mine], pts_send, pts_recv.at[k - 1], x_peers[k - 1])

    def fetch_far():
        for k, rows in ((1, parts[0]), (3, parts[1])):
            landed(pts.at[k - 1, mine], pts_recv.at[k - 1])
            send(pts.at[k - 1, rows], pts.at[1, rows], pts_send, pts_recv.at[1], x_peers[k - 1])
            send(pts.at[k - 1, mine], pts.at[k - 1, mine], pair_send, pair_recv, sibling)

    def fetch_end():
        landed(pts.at[1, mine], pts_recv.at[1])
        send(pts.at[1, mine], pts.at[1, mine], pair_send, pair_recv, sibling)
        pending.append((pts.at[:, mine], pts_send))
        pending.append((pts.at[:, mine], pair_send))
        landed(pts.at[:, aligned(half - core * half, half)], pair_recv)

    fetch()
    landed(cx.at[0], cx_recv.at[0])
    vec[1] = merge(vec[0], cx.at[0], NX - 1)
    swap(vec.at[1], z_peers, cz.at[0], vec_send.at[1], cz_recv.at[0], FAR)
    landed(cz.at[0], cz_recv.at[0])
    col_pot = log_mass - merge(vec[1], cz.at[0], NZ - 1)
    wide_pot = to_wide(col_pot, ct)

    def first_rows(r, carry):
        rows = aligned(r * LANES, LANES)
        got = mat[rows, :] + wide_pot
        high = got[:, :LANES]
        for t in range(1, ct):
            high = jnp.maximum(high, got[:, t * LANES : (t + 1) * LANES])
        high = jnp.max(high, axis=1, keepdims=True)
        got = jnp.exp(got - high)
        mat[rows, :] = got
        acc = got[:, :LANES]
        for t in range(1, ct):
            acc += got[:, t * LANES : (t + 1) * LANES]
        part[pl.ds(r, 1), :] = jnp.sum(acc.T, axis=0, keepdims=True)
        top[pl.ds(r, 1), :] = jnp.broadcast_to(high, (LANES, LANES)).T[:1, :]
        return carry

    lax.fori_loop(0, rt, first_rows, 0)
    vec[2] = top[...] + jnp.log(part[...])
    swap(vec.at[2], c_peers, rc.at[0], vec_send.at[2], rc_recv.at[0])
    landed(rc.at[0], rc_recv.at[0])
    row_pot = -merge(vec[2], rc.at[0], NC - 1)
    u = jnp.exp(top[...] + row_pot)
    spread(u, scale, rt)

    for sweep in (1, 2):
        at = 3 * sweep
        vec[at] = column_sums()
        swap(vec.at[at], x_peers, cx.at[sweep], vec_send.at[at], cx_recv.at[sweep])
        landed(cx.at[sweep], cx_recv.at[sweep])
        vec[at + 1] = add_up(vec[at], cx.at[sweep], NX - 1)
        swap(vec.at[at + 1], z_peers, cz.at[sweep], vec_send.at[at + 1], cz_recv.at[sweep], FAR)
        if sweep == 1:
            fetch_far()
        else:
            fetch_end()
            quarter = c_ref[aligned(x * per_x, per_x), :]
            for k in range(NX):
                tile[:, k * npts : (k + 1) * npts] = factor * lax.dot_general(
                    quarter, p_ref[...] if k == 0 else pts[k - 1],
                    (((1,), (1,)), ((), ())), preferred_element_type=f32,
                )
            landed(px.at[0], px_recv.at[0])
        landed(cz.at[sweep], cz_recv.at[sweep])
        v = math.exp(log_mass) / add_up(vec[at + 1], cz.at[sweep], NZ - 1)
        row_sums(to_wide(v, ct))
        vec[at + 2] = u * part[...]
        swap(vec.at[at + 2], c_peers, rc.at[sweep], vec_send.at[at + 2], rc_recv.at[sweep])
        if sweep == 2:
            total[...] = col_pot + jnp.log(v)
            spread(total[pl.ds(x * qt, qt), :], cpot, qt)
            for k in range(NX):
                pot = vec[9] if k == 0 else px[0, k - 1]
                for t in range(rt):
                    cols = slice(k * npts + t * LANES, k * npts + (t + 1) * LANES)
                    tile[:, cols] = jnp.exp(tile[:, cols] + (cpot[...] + pot[t : t + 1, :]))
        landed(rc.at[sweep], rc_recv.at[sweep])
        got = add_up(vec[at + 2], rc.at[sweep], NC - 1)
        if sweep == 1:
            u = u / got
            vec[9] = row_pot - jnp.log(got)
            swap(vec.at[9], x_peers, px.at[0], vec_send.at[9], px_recv.at[0])
            spread(u, scale, rt)
        else:
            vec[10] = 1.0 / got
            swap(vec.at[10], x_peers, px.at[1], vec_send.at[10], px_recv.at[1])
            landed(px.at[1], px_recv.at[1])

    mass = jnp.zeros((per_x, LANES), f32)
    acc = jnp.zeros((per_x, depth), f32)
    for k in range(NX):
        by = vec[10] if k == 0 else px[1, k - 1]
        weights = []
        for t in range(rt):
            got = tile[:, k * npts + t * LANES : k * npts + (t + 1) * LANES] * by[t : t + 1, :]
            mass += got
            weights.append(got.astype(jnp.bfloat16))
        acc += jnp.dot(
            jnp.concatenate(weights, axis=1), p_ref[...] if k == 0 else pts[k - 1],
            preferred_element_type=f32,
        )
    num[...] = acc

    def piece(j):
        return num.at[aligned(((z + j) % NZ) * per, per)]

    for t in range(qt):
        mass_out[t : t + 1, :] = jnp.sum(mass[t * LANES : (t + 1) * LANES, :].T, axis=0, keepdims=True)
    swap(mass_out, z_peers, mass_in, mass_send, mass_recv, FAR)
    for j in BY_RELAY:
        by = j - 4 if j < 8 else j + 4
        send(piece(j), nz.at[j - 1], nz_send, nz_recv.at[1 if j < 8 else 2], z_peers[by - 1])
    for j in NEAR:
        send(piece(j), nz.at[j - 1], nz_send, nz_recv.at[0], z_peers[j - 1])
    for j, group, slots in ((4, 1, (5, 6, 7)), (12, 2, (8, 9, 10, 11))):
        landed(nz.at[pl.ds(slots[0] - 1, len(slots))], nz_recv.at[group])
        here = piece(j)
        acc = here[...]
        for i in slots:
            acc += nz[i - 1]
        here[...] = acc
        send(here, nz.at[j - 1], nz_send, nz_recv.at[0], z_peers[j - 1])
    pending.append((nz, nz_send))

    landed(mass_in, mass_recv)
    total[:qt, :] = add_up(mass_out[...], mass_in, NZ - 1)
    row = total[pl.ds(z * per // LANES, 1), :]
    scale[:LANES, :] = jnp.broadcast_to(row, (LANES, LANES)).T
    mass = scale[aligned((z * per) % LANES, per), :][:, :1]

    landed(nz.at[pl.ds(0, 8)], nz_recv.at[0])
    acc = piece(0)[...]
    for j in NEAR + [4, 12]:
        acc += nz[j - 1]
    own = aligned((x * NZ + z) * per, per)
    acc = (acc + c_ref[own, :].astype(f32)) / (mass + 1.0)
    o_ref[own, :] = acc.astype(o_ref.dtype)

    def rows_of(j):
        return o_ref.at[aligned((x * NZ + (z + NZ - j) % NZ) * per, per)]

    def hand_on(rows, recv, peer):
        send(rows, rows, ag_send, recv, peer)

    for j in (4, 12, 1, 15, 2, 14, 3, 13):
        hand_on(rows_of(0), agz_recv.at[j], z_peers[j - 1])

    for j in LANDING:
        rows = rows_of(j)
        if j:
            landed(rows, agz_recv.at[j])
        if j == 4:
            for a in (4, 3, 2, 1):
                hand_on(rows, agz_recv.at[4 + a], z_peers[a - 1])
        if j == 12:
            for a in (3, 2, 1):
                hand_on(rows, agz_recv.at[12 - a], z_peers[NZ - a - 1])
        for peer in (x_peers[1], x_peers[0], x_peers[2]):
            hand_on(rows, agx_recv, peer)
    landed(o_ref.at[pl.ds(0, (NX - 1) * per_x)], agx_recv)
    pending.append((o_ref.at[pl.ds(0, (4 * NZ - 1) * per)], ag_send))

    drain()


def shards(points, centroids):
    npts, depth = points.shape
    ncent = centroids.shape[0]
    n_total = npts * lax.axis_size("dp")
    k_total = ncent * lax.axis_size("cent")
    rt, ct = npts // LANES, ncent // LANES
    per_x, per = ncent // NX, ncent // (NX * NZ)
    f32, bf16 = jnp.float32, jnp.bfloat16
    vmem = pl.BlockSpec(memory_space=pltpu.VMEM)
    hbm = pl.BlockSpec(memory_space=pl.ANY)
    dma = pltpu.SemaphoreType.DMA
    return pl.pallas_call(
        functools.partial(kernel, math.log(n_total / k_total), 1.0 / math.sqrt(depth)),
        out_shape=jax.ShapeDtypeStruct((ncent, depth), bf16),
        in_specs=[hbm, hbm],
        out_specs=vmem,
        scratch_shapes=[
            pltpu.VMEM((npts, depth), bf16),
            pltpu.VMEM((ncent, depth), bf16),
            pltpu.VMEM((NX - 1, npts, depth), bf16),
            pltpu.VMEM((npts, ncent), f32),
            pltpu.VMEM((npts, LANES), f32),
            pltpu.VMEM((per_x, NX * npts), f32),
            pltpu.VMEM((per_x, depth), f32),
            pltpu.VMEM((ct, LANES), f32),
            pltpu.VMEM((rt, LANES), f32),
            pltpu.VMEM((rt, LANES), f32),
            pltpu.VMEM((per_x, LANES), f32),
            pltpu.VMEM((11, ct, LANES), f32),
            pltpu.VMEM((3, NX - 1, ct, LANES), f32),
            pltpu.VMEM((3, NZ - 1, ct, LANES), f32),
            pltpu.VMEM((3, NC - 1, rt, LANES), f32),
            pltpu.VMEM((2, NX - 1, rt, LANES), f32),
            pltpu.VMEM((per_x // LANES, LANES), f32),
            pltpu.VMEM((NZ - 1, per_x // LANES, LANES), f32),
            pltpu.VMEM((NZ - 1, per, depth), f32),
            dma((5,)), dma, dma((NX - 1,)), dma, dma,
            dma((11,)), dma((3,)), dma((3,)), dma((3,)), dma((2,)), dma, dma,
            dma, dma((3,)), dma, dma((NZ,)), dma,
        ],
        compiler_params=pltpu.CompilerParams(
            collective_id=0, has_side_effects=True, vmem_limit_bytes=60 * 2**20
        ),
        cost_estimate=pl.CostEstimate(
            flops=6 * npts * ncent * depth, transcendentals=3 * npts * ncent,
            bytes_accessed=2 * (npts + 2 * ncent) * depth,
        ),
        name="balance",
    )(points, centroids)


def solution(mesh):
    return jax.shard_map(
        shards,
        mesh=mesh,
        in_specs=(P("dp", None), P("cent", None)),
        out_specs=P("cent", None),
        check_vma=False,
    )
```

```python
import functools
import math

import jax
import jax.numpy as jnp
from jax import lax
from jax.experimental import pallas as pl
from jax.experimental.pallas import tpu as pltpu
from jax.sharding import PartitionSpec as P

NX, NZ, NC = 4, 16, 8
LANES = 128
SPAN = 85.0
MESH = pl.DeviceIdType.MESH
FAR = [8, 7, 9, 6, 10, 5, 11, 4, 12, 3, 13, 2, 14, 1, 15]
NEAR = [3, 13, 2, 14, 1, 15]
BY_RELAY = [8, 9, 7, 10, 6, 11, 5]
LANDING = [0, 4, 12, 1, 15, 2, 14, 3, 13, 5, 11, 6, 10, 7, 9, 8]


def aligned(start, size):
    return pl.ds(pl.multiple_of(start, size), size)


def to_rows(wide, tiles):
    return jnp.concatenate(
        [wide[:, t * LANES : (t + 1) * LANES] for t in range(tiles)], axis=0
    )


def to_wide(rows, tiles):
    return jnp.concatenate([rows[t : t + 1, :] for t in range(tiles)], axis=1)


def coded(value, mass):
    most = jnp.max(jnp.abs(value), axis=1, keepdims=True)
    scale = jnp.maximum(most * 1.01, 1e-30).astype(jnp.bfloat16).astype(jnp.float32)
    power = jnp.exp(jnp.abs(value) * (2.0 * SPAN / scale) - SPAN)
    power = jnp.where(value < 0.0, -power, power)
    high = mass.astype(jnp.bfloat16).astype(jnp.float32)
    middle = (mass - high).astype(jnp.bfloat16).astype(jnp.float32)
    lane = lax.broadcasted_iota(jnp.int32, (value.shape[0], LANES), 1)
    more = jnp.where(lane == 0, scale, jnp.where(lane == 1, high, jnp.where(lane == 2, middle, mass - high - middle)))
    return jnp.concatenate([power, more], axis=1).astype(jnp.bfloat16)


def decoded(piece):
    depth = piece.shape[1] - LANES
    power = piece[:, :depth].astype(jnp.float32)
    more = piece[:, depth:].astype(jnp.float32)
    value = (jnp.log(jnp.abs(power)) + SPAN) * (more[:, :1] * (0.5 / SPAN))
    mass = more[:, 1:2] + more[:, 2:3] + more[:, 3:4]
    return jnp.where(power < 0.0, -value, value), mass


def kernel(
    log_mass, factor,
    p_hbm, c_hbm, o_ref,
    p_ref, c_ref, pts, mat, scale, tile, num, masses, total, part, top, cpot,
    vec, cx, cz, rc, px, code, nz,
    in_sem, pts_send, pts_recv, pair_send, pair_recv,
    vec_send, cx_recv, cz_recv, rc_recv, px_recv,
    nz_send, nz_recv, ag_send, agz_recv, agx_recv,
):
    npts, depth = p_ref.shape
    ncent = c_ref.shape[0]
    rt, ct = npts // LANES, ncent // LANES
    per_x, per = ncent // NX, ncent // (NX * NZ)
    qt = per_x // LANES
    half = npts // 2
    f32 = jnp.float32

    dp = lax.axis_index("dp")
    cent = lax.axis_index("cent")
    x, z = dp // NZ, dp % NZ
    core = cent % 2

    def x_peer(k):
        return {"dp": ((x + k) % NX) * NZ + z}

    def z_peer(k):
        return {"dp": x * NZ + (z + k) % NZ}

    def c_peer(k):
        return {"cent": (cent + k) % NC}

    sibling = {"cent": cent + 1 - 2 * core}
    x_peers = [x_peer(k) for k in range(1, NX)]
    z_peers = [z_peer(k) for k in range(1, NZ)]
    c_peers = [c_peer(k) for k in range(1, NC)]

    c_in = pltpu.make_async_copy(c_hbm, c_ref, in_sem.at[4])
    c_in.start()
    p_in = []
    for r in range(4):
        rows = pl.ds(r * (npts // 4), npts // 4)
        p_in.append(pltpu.make_async_copy(p_hbm.at[rows], p_ref.at[rows], in_sem.at[r]))
        p_in[-1].start()

    barrier = pltpu.get_barrier_semaphore()
    for peer in x_peers + z_peers + c_peers:
        pl.semaphore_signal(barrier, inc=1, device_id=peer, device_id_type=MESH)

    pending = []

    def send(src, dst, send_sem, recv_sem, peer):
        pltpu.make_async_remote_copy(
            src_ref=src, dst_ref=dst, send_sem=send_sem, recv_sem=recv_sem,
            device_id=peer, device_id_type=MESH,
        ).start()

    def landed(land, recv):
        pltpu.make_async_copy(land, land, recv).wait()

    def drain():
        for land, sem in pending:
            landed(land, sem)

    def swap(src, peers, land, send_sem, recv, order=None):
        for k in order or range(1, len(peers) + 1):
            send(src, land.at[k - 1], send_sem, recv, peers[k - 1])
        pending.append((land, send_sem))

    def merge(own, land, count):
        peak = own
        for k in range(count):
            peak = jnp.maximum(peak, land[k])
        acc = jnp.exp(own - peak)
        for k in range(count):
            acc += jnp.exp(land[k] - peak)
        return peak + jnp.log(acc)

    def add_up(own, land, count):
        acc = own
        for k in range(count):
            acc += land[k]
        return acc

    def spread(rows, out, tiles):
        for t in range(tiles):
            wide = jnp.broadcast_to(rows[t : t + 1, :], (LANES, LANES))
            out[t * LANES : (t + 1) * LANES, :] = wide.T

    def column_sums():
        def step(r, acc):
            rows = aligned(r * LANES, LANES)
            by = scale[rows, :]
            out = []
            for t in range(ct):
                v = mat[rows, t * LANES : (t + 1) * LANES] * by
                out.append(acc[t] + jnp.sum(v.reshape(LANES // 8, 8, LANES), axis=0))
            return tuple(out)

        zero = tuple(jnp.zeros((8, LANES), f32) for _ in range(ct))
        acc = lax.fori_loop(0, rt, step, zero)
        return jnp.concatenate([jnp.sum(a, axis=0, keepdims=True) for a in acc], axis=0)

    def row_sums(wide):
        def step(r, carry):
            rows = aligned(r * LANES, LANES)
            acc = mat[rows, :LANES] * wide[:, :LANES]
            for t in range(1, ct):
                acc += mat[rows, t * LANES : (t + 1) * LANES] * wide[:, t * LANES : (t + 1) * LANES]
            part[pl.ds(r, 1), :] = jnp.sum(acc.T, axis=0, keepdims=True)
            return carry

        lax.fori_loop(0, rt, step, 0)

    c_in.wait()
    peak8 = jnp.full((8, ncent), -jnp.inf, f32)
    for r in range(4):
        p_in[r].wait()
        rows = pl.ds(r * (npts // 4), npts // 4)
        got = factor * lax.dot_general(
            p_ref[rows, :], c_ref[...], (((1,), (1,)), ((), ())), preferred_element_type=f32
        )
        mat[rows, :] = got
        peak8 = jnp.maximum(peak8, jnp.max(got.reshape(npts // 32, 8, ncent), axis=0))
    peak = jnp.max(peak8, axis=0, keepdims=True)

    def first_sum(r, acc):
        rows = aligned(r * LANES, LANES)
        got = jnp.exp(mat[rows, :] - peak)
        return acc + jnp.sum(got.reshape(LANES // 8, 8, ncent), axis=0)

    acc = lax.fori_loop(0, rt, first_sum, jnp.zeros((8, ncent), f32))
    vec[0] = to_rows(peak + jnp.log(jnp.sum(acc, axis=0, keepdims=True)), ct)

    pl.semaphore_wait(barrier, NX + NZ + NC - 3)

    swap(vec.at[0], x_peers, cx.at[0], vec_send.at[0], cx_recv.at[0])

    mine = aligned(core * half, half)
    parts = (aligned(core * half, half // 2), aligned(core * half + half // 2, half // 2))

    def fetch():
        for k in (1, 3):
            send(p_ref.at[mine], pts.at[k - 1, mine], pts_send, pts_recv.at[k - 1], x_peers[k - 1])

    def fetch_far():
        for k, rows in ((1, parts[0]), (3, parts[1])):
            landed(pts.at[k - 1, mine], pts_recv.at[k - 1])
            send(pts.at[k - 1, rows], pts.at[1, rows], pts_send, pts_recv.at[1], x_peers[k - 1])
            send(pts.at[k - 1, mine], pts.at[k - 1, mine], pair_send, pair_recv, sibling)

    def fetch_end():
        landed(pts.at[1, mine], pts_recv.at[1])
        send(pts.at[1, mine], pts.at[1, mine], pair_send, pair_recv, sibling)
        pending.append((pts.at[:, mine], pts_send))
        pending.append((pts.at[:, mine], pair_send))
        landed(pts.at[:, aligned(half - core * half, half)], pair_recv)

    fetch()
    landed(cx.at[0], cx_recv.at[0])
    vec[1] = merge(vec[0], cx.at[0], NX - 1)
    swap(vec.at[1], z_peers, cz.at[0], vec_send.at[1], cz_recv.at[0], FAR)
    landed(cz.at[0], cz_recv.at[0])
    col_pot = log_mass - merge(vec[1], cz.at[0], NZ - 1)
    wide_pot = to_wide(col_pot, ct)

    def first_rows(r, carry):
        rows = aligned(r * LANES, LANES)
        got = mat[rows, :] + wide_pot
        high = got[:, :LANES]
        for t in range(1, ct):
            high = jnp.maximum(high, got[:, t * LANES : (t + 1) * LANES])
        high = jnp.max(high, axis=1, keepdims=True)
        got = jnp.exp(got - high)
        mat[rows, :] = got
        acc = got[:, :LANES]
        for t in range(1, ct):
            acc += got[:, t * LANES : (t + 1) * LANES]
        part[pl.ds(r, 1), :] = jnp.sum(acc.T, axis=0, keepdims=True)
        top[pl.ds(r, 1), :] = jnp.broadcast_to(high, (LANES, LANES)).T[:1, :]
        return carry

    lax.fori_loop(0, rt, first_rows, 0)
    vec[2] = top[...] + jnp.log(part[...])
    swap(vec.at[2], c_peers, rc.at[0], vec_send.at[2], rc_recv.at[0])
    landed(rc.at[0], rc_recv.at[0])
    row_pot = -merge(vec[2], rc.at[0], NC - 1)
    u = jnp.exp(top[...] + row_pot)
    spread(u, scale, rt)

    for sweep in (1, 2):
        at = 3 * sweep
        vec[at] = column_sums()
        swap(vec.at[at], x_peers, cx.at[sweep], vec_send.at[at], cx_recv.at[sweep])
        landed(cx.at[sweep], cx_recv.at[sweep])
        vec[at + 1] = add_up(vec[at], cx.at[sweep], NX - 1)
        swap(vec.at[at + 1], z_peers, cz.at[sweep], vec_send.at[at + 1], cz_recv.at[sweep], FAR)
        if sweep == 1:
            fetch_far()
        else:
            fetch_end()
            quarter = c_ref[aligned(x * per_x, per_x), :]
            for k in range(NX):
                tile[:, k * npts : (k + 1) * npts] = factor * lax.dot_general(
                    quarter, p_ref[...] if k == 0 else pts[k - 1],
                    (((1,), (1,)), ((), ())), preferred_element_type=f32,
                )
            landed(px.at[0], px_recv.at[0])
        landed(cz.at[sweep], cz_recv.at[sweep])
        v = math.exp(log_mass) / add_up(vec[at + 1], cz.at[sweep], NZ - 1)
        row_sums(to_wide(v, ct))
        vec[at + 2] = u * part[...]
        swap(vec.at[at + 2], c_peers, rc.at[sweep], vec_send.at[at + 2], rc_recv.at[sweep])
        if sweep == 2:
            total[...] = col_pot + jnp.log(v)
            spread(total[pl.ds(x * qt, qt), :], cpot, qt)
            for k in range(NX):
                pot = vec[9] if k == 0 else px[0, k - 1]
                for t in range(rt):
                    cols = slice(k * npts + t * LANES, k * npts + (t + 1) * LANES)
                    tile[:, cols] = jnp.exp(tile[:, cols] + (cpot[...] + pot[t : t + 1, :]))
        landed(rc.at[sweep], rc_recv.at[sweep])
        got = add_up(vec[at + 2], rc.at[sweep], NC - 1)
        if sweep == 1:
            u = u / got
            vec[9] = row_pot - jnp.log(got)
            swap(vec.at[9], x_peers, px.at[0], vec_send.at[9], px_recv.at[0])
            spread(u, scale, rt)
        else:
            vec[10] = 1.0 / got
            swap(vec.at[10], x_peers, px.at[1], vec_send.at[10], px_recv.at[1])
            landed(px.at[1], px_recv.at[1])

    mass = jnp.zeros((per_x, LANES), f32)
    acc = jnp.zeros((per_x, depth), f32)
    for k in range(NX):
        by = vec[10] if k == 0 else px[1, k - 1]
        weights = []
        for t in range(rt):
            got = tile[:, k * npts + t * LANES : k * npts + (t + 1) * LANES] * by[t : t + 1, :]
            mass += got
            weights.append(got.astype(jnp.bfloat16))
        acc += jnp.dot(
            jnp.concatenate(weights, axis=1), p_ref[...] if k == 0 else pts[k - 1],
            preferred_element_type=f32,
        )
    num[...] = acc

    def piece(j):
        return aligned(((z + j) % NZ) * per, per)

    def send_piece(j, by, at):
        send(code.at[piece(j)], nz.at[j - 1], nz_send, nz_recv.at[at], z_peers[by - 1])

    def gathered(j, slots):
        rows = piece(j)
        acc, held = num[rows, :], masses[rows, :][:, :1]
        for i in slots:
            value, mass = decoded(nz[i - 1])
            acc += value
            held += mass
        return acc, held

    mass = jnp.sum(mass, axis=1, keepdims=True)
    masses[...] = jnp.broadcast_to(mass, masses.shape)
    code[...] = coded(acc, mass)
    for j in BY_RELAY:
        send_piece(j, j - 4 if j < 8 else j + 4, 1 if j < 8 else 2)
    for j in NEAR:
        send_piece(j, j, 0)
    for j, at, slots in ((4, 1, (5, 6, 7)), (12, 2, (8, 9, 10, 11))):
        landed(nz.at[pl.ds(slots[0] - 1, len(slots))], nz_recv.at[at])
        code[piece(j), :] = coded(*gathered(j, slots))
        send_piece(j, j, 0)
    pending.append((nz, nz_send))

    landed(nz.at[pl.ds(0, 8)], nz_recv.at[0])
    acc, mass = gathered(0, NEAR + [4, 12])
    own = aligned((x * NZ + z) * per, per)
    acc = (acc + c_ref[own, :].astype(f32)) / (mass + 1.0)
    o_ref[own, :] = acc.astype(o_ref.dtype)

    def rows_of(j):
        return o_ref.at[aligned((x * NZ + (z + NZ - j) % NZ) * per, per)]

    def hand_on(rows, recv, peer):
        send(rows, rows, ag_send, recv, peer)

    for j in (4, 12, 1, 15, 2, 14, 3, 13):
        hand_on(rows_of(0), agz_recv.at[j], z_peers[j - 1])

    for j in LANDING:
        rows = rows_of(j)
        if j:
            landed(rows, agz_recv.at[j])
        if j == 4:
            for a in (4, 3, 2, 1):
                hand_on(rows, agz_recv.at[4 + a], z_peers[a - 1])
        if j == 12:
            for a in (3, 2, 1):
                hand_on(rows, agz_recv.at[12 - a], z_peers[NZ - a - 1])
        for peer in (x_peers[1], x_peers[0], x_peers[2]):
            hand_on(rows, agx_recv, peer)
    landed(o_ref.at[pl.ds(0, (NX - 1) * per_x)], agx_recv)
    pending.append((o_ref.at[pl.ds(0, (4 * NZ - 1) * per)], ag_send))

    drain()


def shards(points, centroids):
    npts, depth = points.shape
    ncent = centroids.shape[0]
    n_total = npts * lax.axis_size("dp")
    k_total = ncent * lax.axis_size("cent")
    rt, ct = npts // LANES, ncent // LANES
    per_x, per = ncent // NX, ncent // (NX * NZ)
    f32, bf16 = jnp.float32, jnp.bfloat16
    vmem = pl.BlockSpec(memory_space=pltpu.VMEM)
    hbm = pl.BlockSpec(memory_space=pl.ANY)
    dma = pltpu.SemaphoreType.DMA
    return pl.pallas_call(
        functools.partial(kernel, math.log(n_total / k_total), 1.0 / math.sqrt(depth)),
        out_shape=jax.ShapeDtypeStruct((ncent, depth), bf16),
        in_specs=[hbm, hbm],
        out_specs=vmem,
        scratch_shapes=[
            pltpu.VMEM((npts, depth), bf16),
            pltpu.VMEM((ncent, depth), bf16),
            pltpu.VMEM((NX - 1, npts, depth), bf16),
            pltpu.VMEM((npts, ncent), f32),
            pltpu.VMEM((npts, LANES), f32),
            pltpu.VMEM((per_x, NX * npts), f32),
            pltpu.VMEM((per_x, depth), f32),
            pltpu.VMEM((per_x, LANES), f32),
            pltpu.VMEM((ct, LANES), f32),
            pltpu.VMEM((rt, LANES), f32),
            pltpu.VMEM((rt, LANES), f32),
            pltpu.VMEM((per_x, LANES), f32),
            pltpu.VMEM((11, ct, LANES), f32),
            pltpu.VMEM((3, NX - 1, ct, LANES), f32),
            pltpu.VMEM((3, NZ - 1, ct, LANES), f32),
            pltpu.VMEM((3, NC - 1, rt, LANES), f32),
            pltpu.VMEM((2, NX - 1, rt, LANES), f32),
            pltpu.VMEM((per_x, depth + LANES), bf16),
            pltpu.VMEM((NZ - 1, per, depth + LANES), bf16),
            dma((5,)), dma, dma((NX - 1,)), dma, dma,
            dma((11,)), dma((3,)), dma((3,)), dma((3,)), dma((2,)),
            dma, dma((3,)), dma, dma((NZ,)), dma,
        ],
        compiler_params=pltpu.CompilerParams(
            collective_id=0, has_side_effects=True, vmem_limit_bytes=60 * 2**20
        ),
        cost_estimate=pl.CostEstimate(
            flops=6 * npts * ncent * depth, transcendentals=3 * npts * ncent,
            bytes_accessed=2 * (npts + 2 * ncent) * depth,
        ),
        name="balance",
    )(points, centroids)


def solution(mesh):
    return jax.shard_map(
        shards,
        mesh=mesh,
        in_specs=(P("dp", None), P("cent", None)),
        out_specs=P("cent", None),
        check_vma=False,
    )
```

```python
import functools
import math

import jax
import jax.numpy as jnp
from jax import lax
from jax.experimental import pallas as pl
from jax.experimental.pallas import tpu as pltpu
from jax.sharding import PartitionSpec as P

NX, NZ, NC = 4, 16, 8
LANES = 128
SPAN = 85.0
MESH = pl.DeviceIdType.MESH
FAR = [8, 7, 9, 6, 10, 5, 11, 4, 12, 3, 13, 2, 14, 1, 15]
NEAR = [3, 13, 2, 14, 1, 15]
BY_RELAY = [8, 9, 7, 10, 6, 11, 5]
LANDING = [0, 4, 12, 3, 13, 2, 14, 1, 15, 5, 11, 6, 10, 7, 9, 8]


def aligned(start, size):
    return pl.ds(pl.multiple_of(start, size), size)


def to_rows(wide, tiles):
    return jnp.concatenate(
        [wide[:, t * LANES : (t + 1) * LANES] for t in range(tiles)], axis=0
    )


def to_wide(rows, tiles):
    return jnp.concatenate([rows[t : t + 1, :] for t in range(tiles)], axis=1)


def coded(value, mass):
    most = jnp.max(jnp.abs(value), axis=1, keepdims=True)
    scale = jnp.maximum(most * 1.01, 1e-30).astype(jnp.bfloat16).astype(jnp.float32)
    power = jnp.exp(jnp.abs(value) * (2.0 * SPAN / scale) - SPAN)
    power = jnp.where(value < 0.0, -power, power)
    high = mass.astype(jnp.bfloat16).astype(jnp.float32)
    middle = (mass - high).astype(jnp.bfloat16).astype(jnp.float32)
    lane = lax.broadcasted_iota(jnp.int32, (value.shape[0], LANES), 1)
    more = jnp.where(lane == 0, scale, jnp.where(lane == 1, high, jnp.where(lane == 2, middle, mass - high - middle)))
    return jnp.concatenate([power, more], axis=1).astype(jnp.bfloat16)


def decoded(piece):
    depth = piece.shape[1] - LANES
    power = piece[:, :depth].astype(jnp.float32)
    more = piece[:, depth:].astype(jnp.float32)
    value = (jnp.log(jnp.abs(power)) + SPAN) * (more[:, :1] * (0.5 / SPAN))
    mass = more[:, 1:2] + more[:, 2:3] + more[:, 3:4]
    return jnp.where(power < 0.0, -value, value), mass


def kernel(
    log_mass, factor,
    p_hbm, c_hbm, o_ref,
    p_ref, c_ref, pts, mat, scale, tile, num, masses, total, part, top, cpot,
    vec, cx, cz, rc, px, code, nz,
    in_sem, pts_send, pts_recv, pair_send, pair_recv,
    vec_send, cx_recv, cz_recv, rc_recv, px_recv,
    nz_send, nz_recv, ag_send, agz_recv, agx_recv,
):
    npts, depth = p_ref.shape
    ncent = c_ref.shape[0]
    rt, ct = npts // LANES, ncent // LANES
    per_x, per = ncent // NX, ncent // (NX * NZ)
    qt = per_x // LANES
    half = npts // 2
    f32 = jnp.float32

    dp = lax.axis_index("dp")
    cent = lax.axis_index("cent")
    x, z = dp // NZ, dp % NZ
    core = cent % 2

    def x_peer(k):
        return {"dp": ((x + k) % NX) * NZ + z}

    def z_peer(k):
        return {"dp": x * NZ + (z + k) % NZ}

    def c_peer(k):
        return {"cent": (cent + k) % NC}

    sibling = {"cent": cent + 1 - 2 * core}
    x_peers = [x_peer(k) for k in range(1, NX)]
    z_peers = [z_peer(k) for k in range(1, NZ)]
    c_peers = [c_peer(k) for k in range(1, NC)]

    c_in = pltpu.make_async_copy(c_hbm, c_ref, in_sem.at[4])
    c_in.start()
    p_in = []
    for r in range(4):
        rows = pl.ds(r * (npts // 4), npts // 4)
        p_in.append(pltpu.make_async_copy(p_hbm.at[rows], p_ref.at[rows], in_sem.at[r]))
        p_in[-1].start()

    barrier = pltpu.get_barrier_semaphore()
    for peer in x_peers + z_peers + c_peers:
        pl.semaphore_signal(barrier, inc=1, device_id=peer, device_id_type=MESH)

    pending = []

    def send(src, dst, send_sem, recv_sem, peer):
        pltpu.make_async_remote_copy(
            src_ref=src, dst_ref=dst, send_sem=send_sem, recv_sem=recv_sem,
            device_id=peer, device_id_type=MESH,
        ).start()

    def landed(land, recv):
        pltpu.make_async_copy(land, land, recv).wait()

    def drain():
        for land, sem in pending:
            landed(land, sem)

    def swap(src, peers, land, send_sem, recv, order=None):
        for k in order or range(1, len(peers) + 1):
            send(src, land.at[k - 1], send_sem, recv, peers[k - 1])
        pending.append((land, send_sem))

    def merge(own, land, count):
        peak = own
        for k in range(count):
            peak = jnp.maximum(peak, land[k])
        acc = jnp.exp(own - peak)
        for k in range(count):
            acc += jnp.exp(land[k] - peak)
        return peak + jnp.log(acc)

    def add_up(own, land, count):
        acc = own
        for k in range(count):
            acc += land[k]
        return acc

    def spread(rows, out, tiles):
        for t in range(tiles):
            wide = jnp.broadcast_to(rows[t : t + 1, :], (LANES, LANES))
            out[t * LANES : (t + 1) * LANES, :] = wide.T

    def column_sums():
        def step(r, acc):
            rows = aligned(r * LANES, LANES)
            by = scale[rows, :]
            out = []
            for t in range(ct):
                v = mat[rows, t * LANES : (t + 1) * LANES] * by
                out.append(acc[t] + jnp.sum(v.reshape(LANES // 8, 8, LANES), axis=0))
            return tuple(out)

        zero = tuple(jnp.zeros((8, LANES), f32) for _ in range(ct))
        acc = lax.fori_loop(0, rt, step, zero, unroll=True)
        return jnp.concatenate([jnp.sum(a, axis=0, keepdims=True) for a in acc], axis=0)

    def row_sums(wide):
        def step(r, carry):
            rows = aligned(r * LANES, LANES)
            acc = mat[rows, :LANES] * wide[:, :LANES]
            for t in range(1, ct):
                acc += mat[rows, t * LANES : (t + 1) * LANES] * wide[:, t * LANES : (t + 1) * LANES]
            part[pl.ds(r, 1), :] = jnp.sum(acc.T, axis=0, keepdims=True)
            return carry

        lax.fori_loop(0, rt, step, 0, unroll=True)

    c_in.wait()
    peak8 = jnp.full((8, ncent), -jnp.inf, f32)
    for r in range(4):
        p_in[r].wait()
        rows = pl.ds(r * (npts // 4), npts // 4)
        got = factor * lax.dot_general(
            p_ref[rows, :], c_ref[...], (((1,), (1,)), ((), ())), preferred_element_type=f32
        )
        mat[rows, :] = got
        peak8 = jnp.maximum(peak8, jnp.max(got.reshape(npts // 32, 8, ncent), axis=0))
    peak = jnp.max(peak8, axis=0, keepdims=True)

    def first_sum(r, acc):
        rows = aligned(r * LANES, LANES)
        got = jnp.exp(mat[rows, :] - peak)
        return acc + jnp.sum(got.reshape(LANES // 8, 8, ncent), axis=0)

    acc = lax.fori_loop(0, rt, first_sum, jnp.zeros((8, ncent), f32), unroll=True)
    vec[0] = to_rows(peak + jnp.log(jnp.sum(acc, axis=0, keepdims=True)), ct)

    pl.semaphore_wait(barrier, NX + NZ + NC - 3)

    swap(vec.at[0], x_peers, cx.at[0], vec_send.at[0], cx_recv.at[0])

    mine = aligned(core * half, half)
    parts = (aligned(core * half, half // 2), aligned(core * half + half // 2, half // 2))

    def fetch():
        for k in (1, 3):
            send(p_ref.at[mine], pts.at[k - 1, mine], pts_send, pts_recv.at[k - 1], x_peers[k - 1])

    def fetch_far():
        for k, rows in ((1, parts[0]), (3, parts[1])):
            landed(pts.at[k - 1, mine], pts_recv.at[k - 1])
            send(pts.at[k - 1, rows], pts.at[1, rows], pts_send, pts_recv.at[1], x_peers[k - 1])
            send(pts.at[k - 1, mine], pts.at[k - 1, mine], pair_send, pair_recv, sibling)

    def fetch_end():
        landed(pts.at[1, mine], pts_recv.at[1])
        send(pts.at[1, mine], pts.at[1, mine], pair_send, pair_recv, sibling)
        pending.append((pts.at[:, mine], pts_send))
        pending.append((pts.at[:, mine], pair_send))
        landed(pts.at[:, aligned(half - core * half, half)], pair_recv)

    fetch()
    landed(cx.at[0], cx_recv.at[0])
    vec[1] = merge(vec[0], cx.at[0], NX - 1)
    swap(vec.at[1], z_peers, cz.at[0], vec_send.at[1], cz_recv.at[0], FAR)
    landed(cz.at[0], cz_recv.at[0])
    col_pot = log_mass - merge(vec[1], cz.at[0], NZ - 1)
    wide_pot = to_wide(col_pot, ct)

    def first_rows(r, carry):
        rows = aligned(r * LANES, LANES)
        got = mat[rows, :] + wide_pot
        high = got[:, :LANES]
        for t in range(1, ct):
            high = jnp.maximum(high, got[:, t * LANES : (t + 1) * LANES])
        high = jnp.max(high, axis=1, keepdims=True)
        got = jnp.exp(got - high)
        mat[rows, :] = got
        acc = got[:, :LANES]
        for t in range(1, ct):
            acc += got[:, t * LANES : (t + 1) * LANES]
        part[pl.ds(r, 1), :] = jnp.sum(acc.T, axis=0, keepdims=True)
        top[pl.ds(r, 1), :] = jnp.broadcast_to(high, (LANES, LANES)).T[:1, :]
        return carry

    lax.fori_loop(0, rt, first_rows, 0, unroll=True)
    vec[2] = top[...] + jnp.log(part[...])
    swap(vec.at[2], c_peers, rc.at[0], vec_send.at[2], rc_recv.at[0])
    landed(rc.at[0], rc_recv.at[0])
    row_pot = -merge(vec[2], rc.at[0], NC - 1)
    u = jnp.exp(top[...] + row_pot)
    spread(u, scale, rt)

    for sweep in (1, 2):
        at = 3 * sweep
        vec[at] = column_sums()
        swap(vec.at[at], x_peers, cx.at[sweep], vec_send.at[at], cx_recv.at[sweep])
        landed(cx.at[sweep], cx_recv.at[sweep])
        vec[at + 1] = add_up(vec[at], cx.at[sweep], NX - 1)
        swap(vec.at[at + 1], z_peers, cz.at[sweep], vec_send.at[at + 1], cz_recv.at[sweep], FAR)
        if sweep == 1:
            fetch_far()
        else:
            fetch_end()
            quarter = c_ref[aligned(x * per_x, per_x), :]
            for k in range(NX):
                tile[:, k * npts : (k + 1) * npts] = factor * lax.dot_general(
                    quarter, p_ref[...] if k == 0 else pts[k - 1],
                    (((1,), (1,)), ((), ())), preferred_element_type=f32,
                )
            landed(px.at[0], px_recv.at[0])
        landed(cz.at[sweep], cz_recv.at[sweep])
        v = math.exp(log_mass) / add_up(vec[at + 1], cz.at[sweep], NZ - 1)
        row_sums(to_wide(v, ct))
        vec[at + 2] = u * part[...]
        swap(vec.at[at + 2], c_peers, rc.at[sweep], vec_send.at[at + 2], rc_recv.at[sweep])
        if sweep == 2:
            total[...] = col_pot + jnp.log(v)
            spread(total[pl.ds(x * qt, qt), :], cpot, qt)
            for k in range(NX):
                pot = vec[9] if k == 0 else px[0, k - 1]
                for t in range(rt):
                    cols = slice(k * npts + t * LANES, k * npts + (t + 1) * LANES)
                    tile[:, cols] = jnp.exp(tile[:, cols] + (cpot[...] + pot[t : t + 1, :]))
        landed(rc.at[sweep], rc_recv.at[sweep])
        got = add_up(vec[at + 2], rc.at[sweep], NC - 1)
        if sweep == 1:
            u = u / got
            vec[9] = row_pot - jnp.log(got)
            swap(vec.at[9], x_peers, px.at[0], vec_send.at[9], px_recv.at[0])
            spread(u, scale, rt)
        else:
            vec[10] = 1.0 / got
            swap(vec.at[10], x_peers, px.at[1], vec_send.at[10], px_recv.at[1])
            landed(px.at[1], px_recv.at[1])

    mass = jnp.zeros((per_x, LANES), f32)
    acc = jnp.zeros((per_x, depth), f32)
    for k in range(NX):
        by = vec[10] if k == 0 else px[1, k - 1]
        weights = []
        for t in range(rt):
            got = tile[:, k * npts + t * LANES : k * npts + (t + 1) * LANES] * by[t : t + 1, :]
            mass += got
            weights.append(got.astype(jnp.bfloat16))
        acc += jnp.dot(
            jnp.concatenate(weights, axis=1), p_ref[...] if k == 0 else pts[k - 1],
            preferred_element_type=f32,
        )
    num[...] = acc

    def piece(j):
        return aligned(((z + j) % NZ) * per, per)

    def send_piece(j, by, at):
        send(code.at[piece(j)], nz.at[j - 1], nz_send, nz_recv.at[at], z_peers[by - 1])

    def gathered(j, slots):
        rows = piece(j)
        acc, held = num[rows, :], masses[rows, :][:, :1]
        for i in slots:
            value, mass = decoded(nz[i - 1])
            acc += value
            held += mass
        return acc, held

    mass = jnp.sum(mass, axis=1, keepdims=True)
    masses[...] = jnp.broadcast_to(mass, masses.shape)
    code[...] = coded(acc, mass)
    for j in BY_RELAY:
        send_piece(j, j - 4 if j < 8 else j + 4, 1 if j < 8 else 2)
    for j in NEAR:
        send_piece(j, j, 0)
    for j, at, slots in ((4, 1, (5, 6, 7)), (12, 2, (8, 9, 10, 11))):
        landed(nz.at[pl.ds(slots[0] - 1, len(slots))], nz_recv.at[at])
        code[piece(j), :] = coded(*gathered(j, slots))
        send_piece(j, j, 0)
    pending.append((nz, nz_send))

    landed(nz.at[pl.ds(0, 8)], nz_recv.at[0])
    acc, mass = gathered(0, NEAR + [4, 12])
    own = aligned((x * NZ + z) * per, per)
    acc = (acc + c_ref[own, :].astype(f32)) / (mass + 1.0)
    o_ref[own, :] = acc.astype(o_ref.dtype)

    def rows_of(j):
        return o_ref.at[aligned((x * NZ + (z + NZ - j) % NZ) * per, per)]

    def hand_on(rows, recv, peer):
        send(rows, rows, ag_send, recv, peer)

    for j in (4, 12, 3, 13, 2, 14, 1, 15):
        hand_on(rows_of(0), agz_recv.at[j], z_peers[j - 1])

    for j in LANDING:
        rows = rows_of(j)
        if j:
            landed(rows, agz_recv.at[j])
        if j == 4:
            for a in (4, 3, 2, 1):
                hand_on(rows, agz_recv.at[4 + a], z_peers[a - 1])
        if j == 12:
            for a in (3, 2, 1):
                hand_on(rows, agz_recv.at[12 - a], z_peers[NZ - a - 1])
        for peer in (x_peers[1], x_peers[0], x_peers[2]):
            hand_on(rows, agx_recv, peer)
    landed(o_ref.at[pl.ds(0, (NX - 1) * per_x)], agx_recv)
    pending.append((o_ref.at[pl.ds(0, (4 * NZ - 1) * per)], ag_send))

    drain()


def shards(points, centroids):
    npts, depth = points.shape
    ncent = centroids.shape[0]
    n_total = npts * lax.axis_size("dp")
    k_total = ncent * lax.axis_size("cent")
    rt, ct = npts // LANES, ncent // LANES
    per_x, per = ncent // NX, ncent // (NX * NZ)
    f32, bf16 = jnp.float32, jnp.bfloat16
    vmem = pl.BlockSpec(memory_space=pltpu.VMEM)
    hbm = pl.BlockSpec(memory_space=pl.ANY)
    dma = pltpu.SemaphoreType.DMA
    return pl.pallas_call(
        functools.partial(kernel, math.log(n_total / k_total), 1.0 / math.sqrt(depth)),
        out_shape=jax.ShapeDtypeStruct((ncent, depth), bf16),
        in_specs=[hbm, hbm],
        out_specs=vmem,
        scratch_shapes=[
            pltpu.VMEM((npts, depth), bf16),
            pltpu.VMEM((ncent, depth), bf16),
            pltpu.VMEM((NX - 1, npts, depth), bf16),
            pltpu.VMEM((npts, ncent), f32),
            pltpu.VMEM((npts, LANES), f32),
            pltpu.VMEM((per_x, NX * npts), f32),
            pltpu.VMEM((per_x, depth), f32),
            pltpu.VMEM((per_x, LANES), f32),
            pltpu.VMEM((ct, LANES), f32),
            pltpu.VMEM((rt, LANES), f32),
            pltpu.VMEM((rt, LANES), f32),
            pltpu.VMEM((per_x, LANES), f32),
            pltpu.VMEM((11, ct, LANES), f32),
            pltpu.VMEM((3, NX - 1, ct, LANES), f32),
            pltpu.VMEM((3, NZ - 1, ct, LANES), f32),
            pltpu.VMEM((3, NC - 1, rt, LANES), f32),
            pltpu.VMEM((2, NX - 1, rt, LANES), f32),
            pltpu.VMEM((per_x, depth + LANES), bf16),
            pltpu.VMEM((NZ - 1, per, depth + LANES), bf16),
            dma((5,)), dma, dma((NX - 1,)), dma, dma,
            dma((11,)), dma((3,)), dma((3,)), dma((3,)), dma((2,)),
            dma, dma((3,)), dma, dma((NZ,)), dma,
        ],
        compiler_params=pltpu.CompilerParams(
            collective_id=0, has_side_effects=True, vmem_limit_bytes=52 * 2**20
        ),
        cost_estimate=pl.CostEstimate(
            flops=6 * npts * ncent * depth, transcendentals=3 * npts * ncent,
            bytes_accessed=2 * (npts + 2 * ncent) * depth,
        ),
        name="balance",
    )(points, centroids)


def solution(mesh):
    return jax.shard_map(
        shards,
        mesh=mesh,
        in_specs=(P("dp", None), P("cent", None)),
        out_specs=P("cent", None),
        check_vma=False,
    )
```

```python
import functools
import math

import jax
import jax.numpy as jnp
from jax import lax
from jax.experimental import pallas as pl
from jax.experimental.pallas import tpu as pltpu
from jax.sharding import PartitionSpec as P

NX, NZ, NC = 4, 16, 8
LANES = 128
SPAN = 85.0
MESH = pl.DeviceIdType.MESH
FAR = [8, 7, 9, 6, 10, 5, 11, 4, 12, 3, 13, 2, 14, 1, 15]
FAR_C = [4, 3, 5, 2, 6, 1, 7]
FAR_X = [2, 1, 3]
NEAR = [3, 13, 2, 14, 1, 15]
BY_RELAY = [9, 7, 10, 6, 11, 5]
LAG, RINGED = 8, 22
LANDING = (
    [(0, 0), (1, 0)]
    + [(0, j) for j in (4, 12, 3, 13)]
    + [(1, j) for j in (4, 12)]
    + [(0, j) for j in (2, 14, 1, 15)]
    + [(1, j) for j in (3, 13, 2, 14, 1, 15)]
    + [(h, j) for h in (0, 1) for j in (5, 11, 6, 10, 7, 9, 8)]
)


def aligned(start, size):
    return pl.ds(pl.multiple_of(start, size), size)


def to_rows(wide, tiles):
    return jnp.concatenate(
        [wide[:, t * LANES : (t + 1) * LANES] for t in range(tiles)], axis=0
    )


def to_wide(rows, tiles):
    return jnp.concatenate([rows[t : t + 1, :] for t in range(tiles)], axis=1)


def coded(value, scale):
    power = jnp.exp(jnp.abs(value) * (2.0 * SPAN / scale) - SPAN)
    return jnp.where(value < 0.0, -power, power).astype(jnp.bfloat16)


def decoded(power, scale):
    power = power.astype(jnp.float32)
    value = (jnp.log(jnp.abs(power)) + SPAN) * (scale * (0.5 / SPAN))
    return jnp.where(power < 0.0, -value, value)


def scale_of(most):
    return jnp.maximum(most * 1.01, 1e-30).astype(jnp.bfloat16).astype(jnp.float32)


def further(scale, mass):
    high = mass.astype(jnp.bfloat16).astype(jnp.float32)
    middle = (mass - high).astype(jnp.bfloat16).astype(jnp.float32)
    lane = lax.broadcasted_iota(jnp.int32, (mass.shape[0], LANES), 1)
    more = jnp.where(lane == 0, scale, jnp.where(lane == 1, high, jnp.where(lane == 2, middle, mass - high - middle)))
    return more.astype(jnp.bfloat16)


def kernel(
    log_mass, factor,
    p_hbm, c_hbm, o_ref,
    p_ref, c_ref, pts, mat, scale, tile, num, masses, scales, total, part, top, cpot,
    vec, cx, cz, rc, px, code_a, code_b, nz_a, nz_b,
    in_sem, pts_send, pts_recv, pair_send, pair_recv,
    vec_send, cx_recv, cz_recv, rc_recv, px_recv,
    nz_send, nz_recv, ag_send, agz_recv, agx_recv, agn_recv,
):
    npts, depth = p_ref.shape
    ncent = c_ref.shape[0]
    rt, ct = npts // LANES, ncent // LANES
    per_x, per = ncent // NX, ncent // (NX * NZ)
    qt = per_x // LANES
    half = npts // 2
    f32 = jnp.float32

    dp = lax.axis_index("dp")
    cent = lax.axis_index("cent")
    x, z = dp // NZ, dp % NZ
    core = cent % 2

    def x_peer(k):
        return {"dp": ((x + k) % NX) * NZ + z}

    def z_peer(k):
        return {"dp": x * NZ + (z + k) % NZ}

    def c_peer(k):
        return {"cent": (cent + k) % NC}

    sibling = {"cent": cent + 1 - 2 * core}
    x_peers = [x_peer(k) for k in range(1, NX)]
    z_peers = [z_peer(k) for k in range(1, NZ)]
    c_peers = [c_peer(k) for k in range(1, NC)]

    c_in = pltpu.make_async_copy(c_hbm, c_ref, in_sem.at[4])
    c_in.start()
    p_in = []
    for r in range(4):
        rows = pl.ds(r * (npts // 4), npts // 4)
        p_in.append(pltpu.make_async_copy(p_hbm.at[rows], p_ref.at[rows], in_sem.at[r]))
        p_in[-1].start()

    barrier = pltpu.get_barrier_semaphore()
    for peer in x_peers + z_peers + c_peers:
        pl.semaphore_signal(barrier, inc=1, device_id=peer, device_id_type=MESH)

    pending = []

    def on_core(which, go):
        pl.when(core == which)(go)

    def send(src, dst, send_sem, recv_sem, peer):
        pltpu.make_async_remote_copy(
            src_ref=src, dst_ref=dst, send_sem=send_sem, recv_sem=recv_sem,
            device_id=peer, device_id_type=MESH,
        ).start()

    def landed(land, recv):
        pltpu.make_async_copy(land, land, recv).wait()

    def drain():
        for land, sem in pending:
            landed(land, sem)

    def swap(src, peers, land, send_sem, recv, order=None):
        for k in order or range(1, len(peers) + 1):
            send(src, land.at[k - 1], send_sem, recv, peers[k - 1])
        pending.append((land, send_sem))

    def merge(own, land, count):
        peak = own
        for k in range(count):
            peak = jnp.maximum(peak, land[k])
        acc = jnp.exp(own - peak)
        for k in range(count):
            acc += jnp.exp(land[k] - peak)
        return peak + jnp.log(acc)

    def add_up(own, land, count):
        acc = own
        for k in range(count):
            acc += land[k]
        return acc

    def spread(rows, out, tiles):
        for t in range(tiles):
            wide = jnp.broadcast_to(rows[t : t + 1, :], (LANES, LANES))
            out[t * LANES : (t + 1) * LANES, :] = wide.T

    def column_sums():
        def step(r, acc):
            rows = aligned(r * LANES, LANES)
            by = scale[rows, :]
            out = []
            for t in range(ct):
                v = mat[rows, t * LANES : (t + 1) * LANES] * by
                out.append(acc[t] + jnp.sum(v.reshape(LANES // 8, 8, LANES), axis=0))
            return tuple(out)

        zero = tuple(jnp.zeros((8, LANES), f32) for _ in range(ct))
        acc = lax.fori_loop(0, rt, step, zero, unroll=True)
        return jnp.concatenate([jnp.sum(a, axis=0, keepdims=True) for a in acc], axis=0)

    def row_sums(wide):
        def step(r, carry):
            rows = aligned(r * LANES, LANES)
            acc = mat[rows, :LANES] * wide[:, :LANES]
            for t in range(1, ct):
                acc += mat[rows, t * LANES : (t + 1) * LANES] * wide[:, t * LANES : (t + 1) * LANES]
            part[pl.ds(r, 1), :] = jnp.sum(acc.T, axis=0, keepdims=True)
            return carry

        lax.fori_loop(0, rt, step, 0, unroll=True)

    c_in.wait()
    peak8 = jnp.full((8, ncent), -jnp.inf, f32)
    for r in range(4):
        p_in[r].wait()
        rows = pl.ds(r * (npts // 4), npts // 4)
        got = factor * lax.dot_general(
            p_ref[rows, :], c_ref[...], (((1,), (1,)), ((), ())), preferred_element_type=f32
        )
        mat[rows, :] = got
        peak8 = jnp.maximum(peak8, jnp.max(got.reshape(npts // 32, 8, ncent), axis=0))
    peak = jnp.max(peak8, axis=0, keepdims=True)

    def first_sum(r, acc):
        rows = aligned(r * LANES, LANES)
        got = jnp.exp(mat[rows, :] - peak)
        return acc + jnp.sum(got.reshape(LANES // 8, 8, ncent), axis=0)

    acc = lax.fori_loop(0, rt, first_sum, jnp.zeros((8, ncent), f32), unroll=True)
    vec[0] = to_rows(peak + jnp.log(jnp.sum(acc, axis=0, keepdims=True)), ct)

    pl.semaphore_wait(barrier, NX + NZ + NC - 3)

    swap(vec.at[0], x_peers, cx.at[0], vec_send.at[0], cx_recv.at[0], FAR_X)

    mine = aligned(core * half, half)
    parts = (aligned(core * half, half // 2), aligned(core * half + half // 2, half // 2))

    def fetch():
        for k in (1, 3):
            send(p_ref.at[mine], pts.at[k - 1, mine], pts_send, pts_recv.at[k - 1], x_peers[k - 1])

    def fetch_far():
        for k, rows in ((1, parts[0]), (3, parts[1])):
            landed(pts.at[k - 1, mine], pts_recv.at[k - 1])
            send(pts.at[k - 1, rows], pts.at[1, rows], pts_send, pts_recv.at[1], x_peers[k - 1])
            send(pts.at[k - 1, mine], pts.at[k - 1, mine], pair_send, pair_recv, sibling)

    def fetch_end():
        landed(pts.at[1, mine], pts_recv.at[1])
        send(pts.at[1, mine], pts.at[1, mine], pair_send, pair_recv, sibling)
        pending.append((pts.at[:, mine], pts_send))
        pending.append((pts.at[:, mine], pair_send))
        landed(pts.at[:, aligned(half - core * half, half)], pair_recv)

    fetch()
    landed(cx.at[0], cx_recv.at[0])
    vec[1] = merge(vec[0], cx.at[0], NX - 1)
    swap(vec.at[1], z_peers, cz.at[0], vec_send.at[1], cz_recv.at[0], FAR)
    landed(cz.at[0], cz_recv.at[0])
    col_pot = log_mass - merge(vec[1], cz.at[0], NZ - 1)
    wide_pot = to_wide(col_pot, ct)

    def first_rows(r, carry):
        rows = aligned(r * LANES, LANES)
        got = mat[rows, :] + wide_pot
        high = got[:, :LANES]
        for t in range(1, ct):
            high = jnp.maximum(high, got[:, t * LANES : (t + 1) * LANES])
        high = jnp.max(high, axis=1, keepdims=True)
        got = jnp.exp(got - high)
        mat[rows, :] = got
        acc = got[:, :LANES]
        for t in range(1, ct):
            acc += got[:, t * LANES : (t + 1) * LANES]
        part[pl.ds(r, 1), :] = jnp.sum(acc.T, axis=0, keepdims=True)
        top[pl.ds(r, 1), :] = jnp.broadcast_to(high, (LANES, LANES)).T[:1, :]
        return carry

    lax.fori_loop(0, rt, first_rows, 0, unroll=True)
    vec[2] = top[...] + jnp.log(part[...])
    swap(vec.at[2], c_peers, rc.at[0], vec_send.at[2], rc_recv.at[0], FAR_C)
    landed(rc.at[0], rc_recv.at[0])
    row_pot = -merge(vec[2], rc.at[0], NC - 1)
    u = jnp.exp(top[...] + row_pot)
    spread(u, scale, rt)

    for sweep in (1, 2):
        at = 3 * sweep
        vec[at] = column_sums()
        swap(vec.at[at], x_peers, cx.at[sweep], vec_send.at[at], cx_recv.at[sweep], FAR_X)
        landed(cx.at[sweep], cx_recv.at[sweep])
        vec[at + 1] = add_up(vec[at], cx.at[sweep], NX - 1)
        swap(vec.at[at + 1], z_peers, cz.at[sweep], vec_send.at[at + 1], cz_recv.at[sweep], FAR)
        if sweep == 1:
            fetch_far()
        else:
            fetch_end()
            quarter = c_ref[aligned(x * per_x, per_x), :]
            for k in range(NX):
                tile[:, k * npts : (k + 1) * npts] = factor * lax.dot_general(
                    quarter, p_ref[...] if k == 0 else pts[k - 1],
                    (((1,), (1,)), ((), ())), preferred_element_type=f32,
                )
            landed(px.at[0], px_recv.at[0])
        landed(cz.at[sweep], cz_recv.at[sweep])
        v = math.exp(log_mass) / add_up(vec[at + 1], cz.at[sweep], NZ - 1)
        row_sums(to_wide(v, ct))
        vec[at + 2] = u * part[...]
        swap(vec.at[at + 2], c_peers, rc.at[sweep], vec_send.at[at + 2], rc_recv.at[sweep], FAR_C)
        if sweep == 2:
            total[...] = col_pot + jnp.log(v)
            spread(total[pl.ds(x * qt, qt), :], cpot, qt)
            for k in range(NX):
                pot = vec[9] if k == 0 else px[0, k - 1]
                for t in range(rt):
                    cols = slice(k * npts + t * LANES, k * npts + (t + 1) * LANES)
                    tile[:, cols] = jnp.exp(tile[:, cols] + (cpot[...] + pot[t : t + 1, :]))
        landed(rc.at[sweep], rc_recv.at[sweep])
        got = add_up(vec[at + 2], rc.at[sweep], NC - 1)
        if sweep == 1:
            u = u / got
            vec[9] = row_pot - jnp.log(got)
            swap(vec.at[9], x_peers, px.at[0], vec_send.at[9], px_recv.at[0])
            spread(u, scale, rt)
        else:
            vec[10] = 1.0 / got
            swap(vec.at[10], x_peers, px.at[1], vec_send.at[10], px_recv.at[1], FAR_X)
            landed(px.at[1], px_recv.at[1])

    mass = jnp.zeros((per_x, LANES), f32)
    acc = jnp.zeros((per_x, depth), f32)
    for k in range(NX):
        by = vec[10] if k == 0 else px[1, k - 1]
        weights = []
        for t in range(rt):
            got = tile[:, k * npts + t * LANES : k * npts + (t + 1) * LANES] * by[t : t + 1, :]
            mass += got
            weights.append(got.astype(jnp.bfloat16))
        acc += jnp.dot(
            jnp.concatenate(weights, axis=1), p_ref[...] if k == 0 else pts[k - 1],
            preferred_element_type=f32,
        )
    num[...] = acc

    width = depth // 2
    codes, lands = (code_a, code_b), (nz_a, nz_b)

    def columns(h):
        return slice(h * width, (h + 1) * width)

    def piece(j):
        return aligned(((z + j) % NZ) * per, per)

    def send_piece(h, j, by, at):
        send(codes[h].at[piece(j)], lands[h].at[j - 1], nz_send.at[h], nz_recv.at[h, at], z_peers[by - 1])

    def scale_in(i):
        return nz_a[i - 1, :, width : width + 1].astype(f32)

    def gathered(h, j, slots):
        acc = num[piece(j), columns(h)]
        for i in slots:
            acc += decoded(lands[h][i - 1, :, :width], scale_in(i))
        return acc

    def gathered_mass(j, slots):
        held = masses[piece(j), :][:, :1]
        for i in slots:
            held += mass_in(i)
        return held

    def mass_in(i):
        more = nz_a[i - 1, :, width:].astype(f32)
        return more[:, 1:2] + more[:, 2:3] + more[:, 3:4]

    mass = jnp.sum(mass, axis=1, keepdims=True)
    masses[...] = jnp.broadcast_to(mass, masses.shape)
    row_scale = scale_of(jnp.max(jnp.abs(acc), axis=1, keepdims=True))
    scales[...] = jnp.broadcast_to(row_scale, scales.shape)
    code_a[:, :width] = coded(acc[:, :width], row_scale)
    code_a[:, width:] = further(row_scale, mass)

    def send_far(h):
        on_core(0, lambda: send_piece(h, 8, 12, 3))
        on_core(1, lambda: send_piece(h, 8, 4, 3))
        for j in BY_RELAY:
            send_piece(h, j, j - 4 if j < 8 else j + 4, 1 if j < 8 else 2)

    send_far(0)
    code_b[...] = coded(acc[:, width:], row_scale)
    send_far(1)
    for h in range(2):
        for j in NEAR:
            send_piece(h, j, j, 0)
        landed(lands[h].at[7], nz_recv.at[h, 3])
        for j, at, slots in ((4, 1, (5, 6, 7)), (12, 2, (9, 10, 11))):
            far = (core == (1 if j == 4 else 0)).astype(f32)
            landed(lands[h].at[pl.ds(slots[0] - 1, len(slots))], nz_recv.at[h, at])
            if h == 0:
                most = scales[piece(j), :][:, :1] + far * scale_in(8)
                for i in slots:
                    most += scale_in(i)
                most = scale_of(most)
                scales[piece(j), :] = jnp.broadcast_to(most, (per, LANES))
                code_a[piece(j), width:] = further(most, gathered_mass(j, slots) + far * mass_in(8))
            codes[h][piece(j), :width] = coded(
                gathered(h, j, slots) + far * decoded(lands[h][7, :, :width], scale_in(8)), scales[piece(j), :][:, :1]
            )
            send_piece(h, j, j, 0)
        pending.append((lands[h], nz_send.at[h]))

    def rows_of(h, j):
        return o_ref.at[aligned((x * NZ + (z + NZ - j) % NZ) * per, per), pl.ds(h * width, width)]

    def hand_on(rows, recv, peer):
        send(rows, rows, ag_send, recv, peer)

    def rows_x(n, i):
        h, j = LANDING[n]
        return o_ref.at[
            aligned((((x + i) % NX) * NZ + (z + NZ - j) % NZ) * per, per), pl.ds(h * width, width)
        ]

    def hand_x(n):
        rows = rows_x(n, 0)
        if n >= RINGED:
            hand_on(rows, agx_recv, x_peers[1])
        hand_on(rows, agx_recv if n % 2 or n >= RINGED else agn_recv.at[n], x_peers[0])
        hand_on(rows, agn_recv.at[n] if n % 2 and n < RINGED else agx_recv, x_peers[2])

    def relay_x(n):
        rows = rows_x(n, 1 if n % 2 else 3)
        landed(rows, agn_recv.at[n])
        hand_on(rows, agx_recv, x_peers[2 if n % 2 else 0])

    own = aligned((x * NZ + z) * per, per)
    ends = NEAR + [4, 12]
    for h in range(2):
        landed(lands[h].at[pl.ds(0, 8)], nz_recv.at[h, 0])
        if h == 0:
            mass = gathered_mass(0, ends)
        acc = (gathered(h, 0, ends) + c_ref[own, columns(h)].astype(f32)) / (mass + 1.0)
        o_ref[own, columns(h)] = acc.astype(o_ref.dtype)
        for j in (4, 12, 3, 13, 2, 14, 1, 15):
            hand_on(rows_of(h, 0), agz_recv.at[h, j], z_peers[j - 1])
        hand_x(h)

    for n in range(2, 2 * NZ):
        h, j = LANDING[n]
        rows = rows_of(h, j)
        landed(rows, agz_recv.at[h, j])
        if j == 4:
            on_core(0, lambda: hand_on(rows, agz_recv.at[h, 8], z_peers[3]))
            for a in (3, 2, 1):
                hand_on(rows, agz_recv.at[h, 4 + a], z_peers[a - 1])
        if j == 12:
            on_core(1, lambda: hand_on(rows, agz_recv.at[h, 8], z_peers[NZ - 5]))
            for a in (3, 2, 1):
                hand_on(rows, agz_recv.at[h, 12 - a], z_peers[NZ - a - 1])
        hand_x(n)
        if LAG <= n < LAG + RINGED:
            relay_x(n - LAG)
    landed(o_ref.at[pl.ds(0, (NX - 1) * per_x - RINGED * per // 2)], agx_recv)
    pending.append((o_ref.at[pl.ds(0, (4 * NZ - 1) * per)], ag_send))

    drain()


def shards(points, centroids):
    npts, depth = points.shape
    ncent = centroids.shape[0]
    n_total = npts * lax.axis_size("dp")
    k_total = ncent * lax.axis_size("cent")
    rt, ct = npts // LANES, ncent // LANES
    per_x, per = ncent // NX, ncent // (NX * NZ)
    f32, bf16 = jnp.float32, jnp.bfloat16
    vmem = pl.BlockSpec(memory_space=pltpu.VMEM)
    hbm = pl.BlockSpec(memory_space=pl.ANY)
    dma = pltpu.SemaphoreType.DMA
    return pl.pallas_call(
        functools.partial(kernel, math.log(n_total / k_total), 1.0 / math.sqrt(depth)),
        out_shape=jax.ShapeDtypeStruct((ncent, depth), bf16),
        in_specs=[hbm, hbm],
        out_specs=vmem,
        scratch_shapes=[
            pltpu.VMEM((npts, depth), bf16),
            pltpu.VMEM((ncent, depth), bf16),
            pltpu.VMEM((NX - 1, npts, depth), bf16),
            pltpu.VMEM((npts, ncent), f32),
            pltpu.VMEM((npts, LANES), f32),
            pltpu.VMEM((per_x, NX * npts), f32),
            pltpu.VMEM((per_x, depth), f32),
            pltpu.VMEM((per_x, LANES), f32),
            pltpu.VMEM((per_x, LANES), f32),
            pltpu.VMEM((ct, LANES), f32),
            pltpu.VMEM((rt, LANES), f32),
            pltpu.VMEM((rt, LANES), f32),
            pltpu.VMEM((per_x, LANES), f32),
            pltpu.VMEM((11, ct, LANES), f32),
            pltpu.VMEM((3, NX - 1, ct, LANES), f32),
            pltpu.VMEM((3, NZ - 1, ct, LANES), f32),
            pltpu.VMEM((3, NC - 1, rt, LANES), f32),
            pltpu.VMEM((2, NX - 1, rt, LANES), f32),
            pltpu.VMEM((per_x, depth // 2 + LANES), bf16),
            pltpu.VMEM((per_x, depth // 2), bf16),
            pltpu.VMEM((NZ - 1, per, depth // 2 + LANES), bf16),
            pltpu.VMEM((NZ - 1, per, depth // 2), bf16),
            dma((5,)), dma, dma((NX - 1,)), dma, dma,
            dma((11,)), dma((3,)), dma((3,)), dma((3,)), dma((2,)),
            dma((2,)), dma((2, 4)), dma, dma((2, NZ)), dma, dma((2 * NZ,)),
        ],
        compiler_params=pltpu.CompilerParams(
            collective_id=0, has_side_effects=True, vmem_limit_bytes=52 * 2**20
        ),
        cost_estimate=pl.CostEstimate(
            flops=6 * npts * ncent * depth, transcendentals=3 * npts * ncent,
            bytes_accessed=2 * (npts + 2 * ncent) * depth,
        ),
        name="balance",
    )(points, centroids)


def solution(mesh):
    return jax.shard_map(
        shards,
        mesh=mesh,
        in_specs=(P("dp", None), P("cent", None)),
        out_specs=P("cent", None),
        check_vma=False,
    )
```

```python
import functools
import math

import jax
import jax.numpy as jnp
from jax import lax
from jax.experimental import pallas as pl
from jax.experimental.pallas import tpu as pltpu
from jax.sharding import PartitionSpec as P

NX, NZ, NC = 4, 16, 8
LANES = 128
SPAN = 85.0
MESH = pl.DeviceIdType.MESH
FAR = [8, 7, 9, 6, 10, 5, 11, 4, 12, 3, 13, 2, 14, 1, 15]
FAR_C = [4, 3, 5, 2, 6, 1, 7]
FAR_X = [2, 1, 3]
FAR_BOTH = [k * NC + m for k in FAR_X for m in FAR_C] + [k * NC for k in FAR_X] + FAR_C
NEAR = [3, 13, 2, 14, 1, 15]
BY_RELAY = [9, 7, 10, 6, 11, 5]
LAG, RINGED = 12, 20
LANDING = (
    [(0, 0), (1, 0)]
    + [(0, j) for j in (4, 12, 3, 13)]
    + [(1, j) for j in (4, 12)]
    + [(0, j) for j in (2, 14, 1, 15)]
    + [(1, j) for j in (3, 13, 2, 14, 1, 15)]
    + [(h, j) for h in (0, 1) for j in (6, 10, 5, 11, 7, 9, 8)]
)


def aligned(start, size):
    return pl.ds(pl.multiple_of(start, size), size)


def to_rows(wide, tiles):
    return jnp.concatenate(
        [wide[:, t * LANES : (t + 1) * LANES] for t in range(tiles)], axis=0
    )


def to_wide(rows, tiles):
    return jnp.concatenate([rows[t : t + 1, :] for t in range(tiles)], axis=1)


def coded(value, scale):
    power = jnp.exp(jnp.abs(value) * (2.0 * SPAN / scale) - SPAN)
    return jnp.where(value < 0.0, -power, power).astype(jnp.bfloat16)


def decoded(power, scale):
    power = power.astype(jnp.float32)
    value = (jnp.log(jnp.abs(power)) + SPAN) * (scale * (0.5 / SPAN))
    return jnp.where(power < 0.0, -value, value)


def scale_of(most):
    return jnp.maximum(most * 1.01, 1e-30).astype(jnp.bfloat16).astype(jnp.float32)


def further(scale, mass):
    high = mass.astype(jnp.bfloat16).astype(jnp.float32)
    middle = (mass - high).astype(jnp.bfloat16).astype(jnp.float32)
    lane = lax.broadcasted_iota(jnp.int32, (mass.shape[0], LANES), 1)
    more = jnp.where(lane == 0, scale, jnp.where(lane == 1, high, jnp.where(lane == 2, middle, mass - high - middle)))
    return more.astype(jnp.bfloat16)


def kernel(
    log_mass, factor,
    p_hbm, c_hbm, o_ref,
    p_ref, c_ref, pts, mat, scale, tile, num, masses, scales, total, part, top, cpot,
    vec, cx, cz, rc, rb, px, inverse, code_a, code_b, nz_a, nz_b,
    in_sem, pts_send, pts_recv, pair_send, pair_recv,
    vec_send, cx_recv, cz_recv, rc_recv, px_recv,
    nz_send, nz_recv, ag_send, agz_recv, agx_recv, agn_recv,
):
    npts, depth = p_ref.shape
    ncent = c_ref.shape[0]
    rt, ct = npts // LANES, ncent // LANES
    per_x, per = ncent // NX, ncent // (NX * NZ)
    qt = per_x // LANES
    half = npts // 2
    f32 = jnp.float32

    dp = lax.axis_index("dp")
    cent = lax.axis_index("cent")
    x, z = dp // NZ, dp % NZ
    core = cent % 2

    def x_peer(k):
        return {"dp": ((x + k) % NX) * NZ + z}

    def z_peer(k):
        return {"dp": x * NZ + (z + k) % NZ}

    def c_peer(k):
        return {"cent": (cent + k) % NC}

    sibling = {"cent": cent + 1 - 2 * core}
    x_peers = [x_peer(k) for k in range(1, NX)]
    z_peers = [z_peer(k) for k in range(1, NZ)]
    c_peers = [c_peer(k) for k in range(1, NC)]
    both = [{**x_peer(k), **c_peer(m)} for k in range(NX) for m in range(NC)][1:]

    barrier = pltpu.get_barrier_semaphore()
    for peer in [z_peers[j - 1] for j in FAR] + both:
        pl.semaphore_signal(barrier, inc=1, device_id=peer, device_id_type=MESH)

    c_in = pltpu.make_async_copy(c_hbm, c_ref, in_sem.at[4])
    c_in.start()
    p_in = []
    for r in range(4):
        rows = pl.ds(r * (npts // 4), npts // 4)
        p_in.append(pltpu.make_async_copy(p_hbm.at[rows], p_ref.at[rows], in_sem.at[r]))
        p_in[-1].start()

    pending = []

    def on_core(which, go):
        pl.when(core == which)(go)

    def send(src, dst, send_sem, recv_sem, peer):
        pltpu.make_async_remote_copy(
            src_ref=src, dst_ref=dst, send_sem=send_sem, recv_sem=recv_sem,
            device_id=peer, device_id_type=MESH,
        ).start()

    def landed(land, recv):
        pltpu.make_async_copy(land, land, recv).wait()

    def drain():
        for land, sem in pending:
            landed(land, sem)

    def swap(src, peers, land, send_sem, recv, order=None):
        for k in order or range(1, len(peers) + 1):
            send(src, land.at[k - 1], send_sem, recv, peers[k - 1])
        pending.append((land, send_sem))

    def merge(own, land, count):
        peak = own
        for k in range(count):
            peak = jnp.maximum(peak, land[k])
        acc = jnp.exp(own - peak)
        for k in range(count):
            acc += jnp.exp(land[k] - peak)
        return peak + jnp.log(acc)

    def add_up(own, land, count):
        acc = own
        for k in range(count):
            acc += land[k]
        return acc

    def spread(rows, out, tiles):
        for t in range(tiles):
            wide = jnp.broadcast_to(rows[t : t + 1, :], (LANES, LANES))
            out[t * LANES : (t + 1) * LANES, :] = wide.T

    def column_sums():
        def step(r, acc):
            rows = aligned(r * LANES, LANES)
            by = scale[rows, :]
            out = []
            for t in range(ct):
                v = mat[rows, t * LANES : (t + 1) * LANES] * by
                out.append(acc[t] + jnp.sum(v.reshape(LANES // 8, 8, LANES), axis=0))
            return tuple(out)

        zero = tuple(jnp.zeros((8, LANES), f32) for _ in range(ct))
        acc = lax.fori_loop(0, rt, step, zero, unroll=True)
        return jnp.concatenate([jnp.sum(a, axis=0, keepdims=True) for a in acc], axis=0)

    def row_sums(wide):
        def step(r, carry):
            rows = aligned(r * LANES, LANES)
            acc = mat[rows, :LANES] * wide[:, :LANES]
            for t in range(1, ct):
                acc += mat[rows, t * LANES : (t + 1) * LANES] * wide[:, t * LANES : (t + 1) * LANES]
            part[pl.ds(r, 1), :] = jnp.sum(acc.T, axis=0, keepdims=True)
            return carry

        lax.fori_loop(0, rt, step, 0, unroll=True)

    c_in.wait()
    peak8 = jnp.full((8, ncent), -jnp.inf, f32)
    for r in range(4):
        p_in[r].wait()
        rows = pl.ds(r * (npts // 4), npts // 4)
        got = factor * lax.dot_general(
            p_ref[rows, :], c_ref[...], (((1,), (1,)), ((), ())), preferred_element_type=f32
        )
        mat[rows, :] = got
        peak8 = jnp.maximum(peak8, jnp.max(got.reshape(npts // 32, 8, ncent), axis=0))
    peak = jnp.max(peak8, axis=0, keepdims=True)

    def first_sum(r, acc):
        rows = aligned(r * LANES, LANES)
        got = jnp.exp(mat[rows, :] - peak)
        return acc + jnp.sum(got.reshape(LANES // 8, 8, ncent), axis=0)

    acc = lax.fori_loop(0, rt, first_sum, jnp.zeros((8, ncent), f32), unroll=True)
    vec[0] = to_rows(peak + jnp.log(jnp.sum(acc, axis=0, keepdims=True)), ct)

    pl.semaphore_wait(barrier, NX * NC + NZ - 2)

    swap(vec.at[0], x_peers, cx.at[0], vec_send.at[0], cx_recv.at[0], FAR_X)

    mine = aligned(core * half, half)
    parts = (aligned(core * half, half // 2), aligned(core * half + half // 2, half // 2))

    def fetch():
        for k in (1, 3):
            send(p_ref.at[mine], pts.at[k - 1, mine], pts_send, pts_recv.at[k - 1], x_peers[k - 1])

    def fetch_far():
        for k, rows in ((1, parts[0]), (3, parts[1])):
            landed(pts.at[k - 1, mine], pts_recv.at[k - 1])
            send(pts.at[k - 1, rows], pts.at[1, rows], pts_send, pts_recv.at[1], x_peers[k - 1])
            send(pts.at[k - 1, mine], pts.at[k - 1, mine], pair_send, pair_recv, sibling)

    def fetch_end():
        landed(pts.at[1, mine], pts_recv.at[1])
        send(pts.at[1, mine], pts.at[1, mine], pair_send, pair_recv, sibling)
        pending.append((pts.at[:, mine], pts_send))
        pending.append((pts.at[:, mine], pair_send))
        landed(pts.at[:, aligned(half - core * half, half)], pair_recv)

    fetch()
    landed(cx.at[0], cx_recv.at[0])
    vec[1] = merge(vec[0], cx.at[0], NX - 1)
    swap(vec.at[1], z_peers, cz.at[0], vec_send.at[1], cz_recv.at[0], FAR)
    landed(cz.at[0], cz_recv.at[0])
    col_pot = log_mass - merge(vec[1], cz.at[0], NZ - 1)
    wide_pot = to_wide(col_pot, ct)

    def first_rows(r, carry):
        rows = aligned(r * LANES, LANES)
        got = mat[rows, :] + wide_pot
        high = got[:, :LANES]
        for t in range(1, ct):
            high = jnp.maximum(high, got[:, t * LANES : (t + 1) * LANES])
        high = jnp.max(high, axis=1, keepdims=True)
        got = jnp.exp(got - high)
        mat[rows, :] = got
        acc = got[:, :LANES]
        for t in range(1, ct):
            acc += got[:, t * LANES : (t + 1) * LANES]
        part[pl.ds(r, 1), :] = jnp.sum(acc.T, axis=0, keepdims=True)
        top[pl.ds(r, 1), :] = jnp.broadcast_to(high, (LANES, LANES)).T[:1, :]
        return carry

    lax.fori_loop(0, rt, first_rows, 0, unroll=True)
    vec[2] = top[...] + jnp.log(part[...])
    swap(vec.at[2], c_peers, rc.at[0], vec_send.at[2], rc_recv.at[0], FAR_C)
    landed(rc.at[0], rc_recv.at[0])
    row_pot = -merge(vec[2], rc.at[0], NC - 1)
    u = jnp.exp(top[...] + row_pot)
    spread(u, scale, rt)

    for sweep in (1, 2):
        at = 3 * sweep
        vec[at] = column_sums()
        swap(vec.at[at], x_peers, cx.at[sweep], vec_send.at[at], cx_recv.at[sweep], FAR_X)
        landed(cx.at[sweep], cx_recv.at[sweep])
        vec[at + 1] = add_up(vec[at], cx.at[sweep], NX - 1)
        swap(vec.at[at + 1], z_peers, cz.at[sweep], vec_send.at[at + 1], cz_recv.at[sweep], FAR)
        if sweep == 1:
            fetch_far()
        else:
            fetch_end()
            quarter = c_ref[aligned(x * per_x, per_x), :]
            for k in range(NX):
                tile[:, k * npts : (k + 1) * npts] = factor * lax.dot_general(
                    quarter, p_ref[...] if k == 0 else pts[k - 1],
                    (((1,), (1,)), ((), ())), preferred_element_type=f32,
                )
            landed(px, px_recv)
        landed(cz.at[sweep], cz_recv.at[sweep])
        v = math.exp(log_mass) / add_up(vec[at + 1], cz.at[sweep], NZ - 1)
        row_sums(to_wide(v, ct))
        vec[at + 2] = u * part[...]
        if sweep == 1:
            swap(vec.at[at + 2], c_peers, rc.at[sweep], vec_send.at[at + 2], rc_recv.at[sweep], FAR_C)
        else:
            swap(vec.at[at + 2], both, rb, vec_send.at[at + 2], rc_recv.at[sweep], FAR_BOTH)
        if sweep == 2:
            total[...] = col_pot + jnp.log(v)
            spread(total[pl.ds(x * qt, qt), :], cpot, qt)
            for k in range(NX):
                pot = vec[9] if k == 0 else px[k - 1]
                for t in range(rt):
                    cols = slice(k * npts + t * LANES, k * npts + (t + 1) * LANES)
                    tile[:, cols] = jnp.exp(tile[:, cols] + (cpot[...] + pot[t : t + 1, :]))
        if sweep == 1:
            landed(rc.at[sweep], rc_recv.at[sweep])
            got = add_up(vec[at + 2], rc.at[sweep], NC - 1)
            u = u / got
            vec[9] = row_pot - jnp.log(got)
            swap(vec.at[9], x_peers, px, vec_send.at[9], px_recv)
            spread(u, scale, rt)
        else:
            landed(rb, rc_recv.at[sweep])
            for k in range(NX):
                got = vec[at + 2] if k == 0 else rb[k * NC - 1]
                for m in range(1, NC):
                    got += rb[k * NC + m - 1]
                inverse[k] = 1.0 / got

    mass = jnp.zeros((per_x, LANES), f32)
    acc = jnp.zeros((per_x, depth), f32)
    for k in range(NX):
        by = inverse[k]
        weights = []
        for t in range(rt):
            got = tile[:, k * npts + t * LANES : k * npts + (t + 1) * LANES] * by[t : t + 1, :]
            mass += got
            weights.append(got.astype(jnp.bfloat16))
        acc += jnp.dot(
            jnp.concatenate(weights, axis=1), p_ref[...] if k == 0 else pts[k - 1],
            preferred_element_type=f32,
        )
    num[...] = acc

    width = depth // 2
    codes, lands = (code_a, code_b), (nz_a, nz_b)

    def columns(h):
        return slice(h * width, (h + 1) * width)

    def piece(j):
        return aligned(((z + j) % NZ) * per, per)

    def send_piece(h, j, by, at):
        send(codes[h].at[piece(j)], lands[h].at[j - 1], nz_send.at[h], nz_recv.at[h, at], z_peers[by - 1])

    def scale_in(i):
        return nz_a[i - 1, :, width : width + 1].astype(f32)

    def gathered(h, j, slots):
        acc = num[piece(j), columns(h)]
        for i in slots:
            acc += decoded(lands[h][i - 1, :, :width], scale_in(i))
        return acc

    def gathered_mass(j, slots):
        held = masses[piece(j), :][:, :1]
        for i in slots:
            held += mass_in(i)
        return held

    def mass_in(i):
        more = nz_a[i - 1, :, width:].astype(f32)
        return more[:, 1:2] + more[:, 2:3] + more[:, 3:4]

    mass = jnp.sum(mass, axis=1, keepdims=True)
    masses[...] = jnp.broadcast_to(mass, masses.shape)
    row_scale = scale_of(jnp.max(jnp.abs(acc), axis=1, keepdims=True))
    scales[...] = jnp.broadcast_to(row_scale, scales.shape)
    code_a[:, :width] = coded(acc[:, :width], row_scale)
    code_a[:, width:] = further(row_scale, mass)

    def send_far(h):
        on_core(0, lambda: send_piece(h, 8, 12, 3))
        on_core(1, lambda: send_piece(h, 8, 4, 3))
        for j in BY_RELAY:
            send_piece(h, j, j - 4 if j < 8 else j + 4, 1 if j < 8 else 2)

    send_far(0)
    for j in NEAR:
        send_piece(0, j, j, 0)
    code_b[...] = coded(acc[:, width:], row_scale)
    send_far(1)
    for h in range(2):
        if h == 1:
            for j in NEAR:
                send_piece(h, j, j, 0)
        landed(lands[h].at[7], nz_recv.at[h, 3])
        for j, at, slots in ((4, 1, (5, 6, 7)), (12, 2, (9, 10, 11))):
            far = (core == (1 if j == 4 else 0)).astype(f32)
            landed(lands[h].at[pl.ds(slots[0] - 1, len(slots))], nz_recv.at[h, at])
            if h == 0:
                most = scales[piece(j), :][:, :1] + far * scale_in(8)
                for i in slots:
                    most += scale_in(i)
                most = scale_of(most)
                scales[piece(j), :] = jnp.broadcast_to(most, (per, LANES))
                code_a[piece(j), width:] = further(most, gathered_mass(j, slots) + far * mass_in(8))
            codes[h][piece(j), :width] = coded(
                gathered(h, j, slots) + far * decoded(lands[h][7, :, :width], scale_in(8)), scales[piece(j), :][:, :1]
            )
            send_piece(h, j, j, 0)
        pending.append((lands[h], nz_send.at[h]))

    def rows_of(h, j):
        return o_ref.at[aligned((x * NZ + (z + NZ - j) % NZ) * per, per), pl.ds(h * width, width)]

    def hand_on(rows, recv, peer):
        send(rows, rows, ag_send, recv, peer)

    def rows_x(n, i):
        h, j = LANDING[n]
        return o_ref.at[
            aligned((((x + i) % NX) * NZ + (z + NZ - j) % NZ) * per, per), pl.ds(h * width, width)
        ]

    def hand_x(n):
        rows = rows_x(n, 0)
        if n >= RINGED:
            hand_on(rows, agx_recv, x_peers[1])
        hand_on(rows, agx_recv if n % 2 or n >= RINGED else agn_recv.at[n], x_peers[0])
        hand_on(rows, agn_recv.at[n] if n % 2 and n < RINGED else agx_recv, x_peers[2])

    def relay_x(n):
        rows = rows_x(n, 1 if n % 2 else 3)
        landed(rows, agn_recv.at[n])
        hand_on(rows, agx_recv, x_peers[2 if n % 2 else 0])

    own = aligned((x * NZ + z) * per, per)
    ends = NEAR + [4, 12]
    for h in range(2):
        landed(lands[h].at[pl.ds(0, 8)], nz_recv.at[h, 0])
        if h == 0:
            mass = gathered_mass(0, ends)
        acc = (gathered(h, 0, ends) + c_ref[own, columns(h)].astype(f32)) / (mass + 1.0)
        o_ref[own, columns(h)] = acc.astype(o_ref.dtype)
        for j in (4, 12, 3, 13, 2, 14, 1, 15):
            hand_on(rows_of(h, 0), agz_recv.at[h, j], z_peers[j - 1])
        hand_x(h)

    for n in range(2, 2 * NZ):
        h, j = LANDING[n]
        rows = rows_of(h, j)
        landed(rows, agz_recv.at[h, j])
        for at, way, which in ((4, 1, None), (12, -1, None), (6, 1, 0), (10, -1, 1)):
            if j == at:
                go = functools.partial(hand_on, rows, agz_recv.at[h, j + 2 * way], z_peers[(2 * way) % NZ - 1])
                if which is None:
                    go()
                else:
                    on_core(which, go)
                hand_on(rows, agz_recv.at[h, j + way], z_peers[way % NZ - 1])
        hand_x(n)
        if LAG <= n < LAG + RINGED:
            relay_x(n - LAG)
    landed(o_ref.at[pl.ds(0, (NX - 1) * per_x - RINGED * per // 2)], agx_recv)
    pending.append((o_ref.at[pl.ds(0, (4 * NZ - 1) * per)], ag_send))

    drain()


def shards(points, centroids):
    npts, depth = points.shape
    ncent = centroids.shape[0]
    n_total = npts * lax.axis_size("dp")
    k_total = ncent * lax.axis_size("cent")
    rt, ct = npts // LANES, ncent // LANES
    per_x, per = ncent // NX, ncent // (NX * NZ)
    f32, bf16 = jnp.float32, jnp.bfloat16
    vmem = pl.BlockSpec(memory_space=pltpu.VMEM)
    hbm = pl.BlockSpec(memory_space=pl.ANY)
    dma = pltpu.SemaphoreType.DMA
    return pl.pallas_call(
        functools.partial(kernel, math.log(n_total / k_total), 1.0 / math.sqrt(depth)),
        out_shape=jax.ShapeDtypeStruct((ncent, depth), bf16),
        in_specs=[hbm, hbm],
        out_specs=vmem,
        scratch_shapes=[
            pltpu.VMEM((npts, depth), bf16),
            pltpu.VMEM((ncent, depth), bf16),
            pltpu.VMEM((NX - 1, npts, depth), bf16),
            pltpu.VMEM((npts, ncent), f32),
            pltpu.VMEM((npts, LANES), f32),
            pltpu.VMEM((per_x, NX * npts), f32),
            pltpu.VMEM((per_x, depth), f32),
            pltpu.VMEM((per_x, LANES), f32),
            pltpu.VMEM((per_x, LANES), f32),
            pltpu.VMEM((ct, LANES), f32),
            pltpu.VMEM((rt, LANES), f32),
            pltpu.VMEM((rt, LANES), f32),
            pltpu.VMEM((per_x, LANES), f32),
            pltpu.VMEM((10, ct, LANES), f32),
            pltpu.VMEM((3, NX - 1, ct, LANES), f32),
            pltpu.VMEM((3, NZ - 1, ct, LANES), f32),
            pltpu.VMEM((2, NC - 1, rt, LANES), f32),
            pltpu.VMEM((NX * NC - 1, rt, LANES), f32),
            pltpu.VMEM((NX - 1, rt, LANES), f32),
            pltpu.VMEM((NX, rt, LANES), f32),
            pltpu.VMEM((per_x, depth // 2 + LANES), bf16),
            pltpu.VMEM((per_x, depth // 2), bf16),
            pltpu.VMEM((NZ - 1, per, depth // 2 + LANES), bf16),
            pltpu.VMEM((NZ - 1, per, depth // 2), bf16),
            dma((5,)), dma, dma((NX - 1,)), dma, dma,
            dma((10,)), dma((3,)), dma((3,)), dma((3,)), dma,
            dma((2,)), dma((2, 4)), dma, dma((2, NZ)), dma, dma((2 * NZ,)),
        ],
        compiler_params=pltpu.CompilerParams(
            collective_id=0, has_side_effects=True, vmem_limit_bytes=52 * 2**20
        ),
        cost_estimate=pl.CostEstimate(
            flops=6 * npts * ncent * depth, transcendentals=3 * npts * ncent,
            bytes_accessed=2 * (npts + 2 * ncent) * depth,
        ),
        name="balance",
    )(points, centroids)


def solution(mesh):
    return jax.shard_map(
        shards,
        mesh=mesh,
        in_specs=(P("dp", None), P("cent", None)),
        out_specs=P("cent", None),
        check_vma=False,
    )
```
